128 devices in a mesh: win: 4 (over x_hi, core), chan: 32 (over y, x_lo, z).
Axes of the slice: x: 4 (x_hi: 2, x_lo: 2; x = x_hi * 2 + x_lo), y: 4, z: 4, core: 2. Of those that a mesh axis runs over, the one named last changes fastest.
Arguments:
- source_spectra: bfloat16 [32, 4096, 1024], P('win', 'chan'), may hold values from -6 to 6
- receiver_spectra: bfloat16 [32, 128, 1024], P('win', 'chan'), may hold values from -6 to 6
- quality_mask: int32 [32, 128], P('win', 'chan'), may hold values 0 or 1
- owner_plan: int32 [6], replicated, may hold values from 0 to 31
Outputs:
- correlations: bfloat16 [6, 128, 128, 4096], P(None, None, 'chan', 'win')
The draws below stay inside these ranges and needn't reach their ends.
All inputs are finite; a program needn't handle non-finite values. No bound on the sum of `quality_mask` on one device may be relied on, other than what follows from the above.
Results may differ from the reference program's by a relative error of at most 0.0055.
Values may be sent and summed in bfloat16 or wider, within the bound.
No kernel may reach another device: no remote copies, remote signals or barrier semaphores. Data moves between devices by JAX's collectives and lax.ppermute only.
A program may use at most 128 MiB of HBM per device.

```python
import math
import jax
import jax.numpy as jnp
from jax import lax

FREQ = 512
LAGS = 4096
SRC = 128
STEPS = 6
WINDOWS = 32
CHANNELS = 128
OWNERS = 32
SOURCES = 4096


def plant(entries, stream_key, low, largest):
    spot = [jax.random.randint(jax.random.fold_in(stream_key, axis), (), 0, length) for axis, length in enumerate(entries.shape)]
    longest = entries.shape.index(max(entries.shape))
    neighbour = spot[:longest] + [(spot[longest] + 1) % entries.shape[longest]] + spot[longest + 1:]
    return entries.at[tuple(spot)].set(low).at[tuple(neighbour)].set(largest)


def block_levels(rng, shape, cuts, least, largest):
    def one(axis_at, shards_of):
        draws = jax.random.uniform(jax.random.fold_in(jax.random.fold_in(rng, 6), axis_at), (shards_of,), jnp.float32, least / len(cuts), largest / len(cuts))
        return jnp.repeat(jnp.exp(draws), shape[axis_at] // shards_of).reshape((-1,) + (1,) * (len(shape) - axis_at - 1))

    factor_of = one(*cuts[0])
    for cut in cuts[1:]:
        factor_of = factor_of * one(*cut)
    return factor_of


def bell_draw(own_key, shape, width, limit, pieces=(), held_as=jnp.bfloat16):
    entries = width * jax.random.normal(own_key, shape, jnp.float32)
    if pieces:
        entries = entries * block_levels(own_key, shape, pieces, -0.22, 0.18)
    return jnp.clip(entries, -limit, limit).astype(held_as)


def setup_inputs(seed: int = 0) -> dict:
    splits = jax.random.split(jax.random.key(seed), 5)
    return {
        "source_spectra": bell_draw(splits[0], (WINDOWS, SOURCES, 2 * FREQ), 1.0, 6.0, ((0, 4), (1, 32))),
        "receiver_spectra": bell_draw(splits[1], (WINDOWS, CHANNELS, 2 * FREQ), 1.0, 6.0, ((0, 4), (1, 32))),
        "quality_mask": plant((jax.random.randint(splits[2], (WINDOWS, CHANNELS), 0, 4) < 3).astype(jnp.int32), jax.random.fold_in(splits[2], 1), 0, 1),
        "owner_plan": plant(jax.random.randint(splits[3], (STEPS,), 0, OWNERS), jax.random.fold_in(splits[3], 1), 0, OWNERS - 1).astype(jnp.int32),
    }


def build_table(start, count, bin_count, lag_count, scale):
    rows = jnp.arange(2 * bin_count, dtype=jnp.int32)
    wave = rows % bin_count + bin_count // 8
    shift = jnp.arange(count, dtype=jnp.int32) + start - lag_count // 2
    phase = wave[:, None] * shift[None, :] % (2 * lag_count)
    angle = phase.astype(jnp.float32) * (math.pi / lag_count)
    table = jnp.where(rows[:, None] < bin_count, jnp.cos(angle), -jnp.sin(angle)) * scale
    return table.astype(jnp.bfloat16)

def build_taper(start, count, lag_count):
    position = jnp.arange(count, dtype=jnp.int32) + start
    edge = jnp.minimum(position, lag_count - 1 - position) + 1
    return jnp.minimum(1.0, edge.astype(jnp.float32) / (lag_count // 16))

def reference(source_spectra, receiver_spectra, quality_mask, owner_plan):
    masked = receiver_spectra.astype(jnp.float32) * quality_mask.astype(jnp.float32)[:, :, None]
    rec_real = masked[:, :, :FREQ]
    rec_imag = masked[:, :, FREQ:]
    lag_table = build_table(0, LAGS, FREQ, LAGS, 1.0 / math.sqrt(FREQ * WINDOWS))
    lag_taper = build_taper(0, LAGS, LAGS)

    def contract(form, left, right):
        return jnp.einsum(form, left, right, precision=lax.Precision.HIGHEST)

    def one_step(owner_index):
        first = (owner_index * SRC).astype(jnp.int32)
        source_block = lax.dynamic_slice_in_dim(source_spectra, first, SRC, 1).astype(jnp.float32)
        src_real = source_block[:, :, :FREQ]
        src_imag = source_block[:, :, FREQ:]
        real_part = contract('wkf,wrf->krf', src_real, rec_real) + contract('wkf,wrf->krf', src_imag, rec_imag)
        imag_part = contract('wkf,wrf->krf', src_imag, rec_real) - contract('wkf,wrf->krf', src_real, rec_imag)
        cross_stack = jnp.concatenate([real_part, imag_part], axis=2)
        stack_rounded = cross_stack.astype(jnp.bfloat16)
        flat = jnp.dot(stack_rounded.reshape(SRC * CHANNELS, 2 * FREQ), lag_table, preferred_element_type=jnp.float32)
        return (flat.reshape(SRC, CHANNELS, LAGS) * lag_taper).astype(jnp.bfloat16)
    return lax.map(one_step, owner_plan)
```

```python
import functools
import math

import jax
import jax.numpy as jnp
from jax import lax
from jax.experimental import pallas as pl
from jax.experimental.pallas import tpu as pltpu
from jax.sharding import PartitionSpec as P

LAGS = 4096
STEPS = 6
FREQ = 512
SRC = 128
HOLDERS = 32
LOCAL_WIN = 8
FINE = 8
VMEM_LIMIT = 48 * 1024 * 1024
F32 = jnp.float32
BF16 = jnp.bfloat16
CORE_SWAP = [(0, 1), (1, 0), (2, 3), (3, 2)]
HALF_SWAP = [(0, 2), (1, 3), (2, 0), (3, 1)]


def params():
    return pltpu.CompilerParams(vmem_limit_bytes=VMEM_LIMIT)


def pack_kernel(re_ref, im_ref, rec_re_ref, rec_im_ref, out_ref, tall, small):
    for part, ref in enumerate((re_ref, im_ref)):
        for w in range(LOCAL_WIN):
            tall[pl.ds(part * LOCAL_WIN + w, 128, stride=16), :] = ref[w].astype(F32).T
    for part, ref in enumerate((rec_re_ref, rec_im_ref)):
        block = jnp.concatenate([ref[...], jnp.zeros((96, 128), BF16)], axis=0)
        small[pl.ds(part, 128, stride=2), :] = block.astype(F32).T
    out_ref[:, :, :128, :] = tall[...].reshape(8, 2, 128, 128).astype(BF16)
    out_ref[:, :, 128:, :] = small[...].reshape(8, 2, 16, 128).astype(BF16)


def pack(source_spectra, masked):
    spec_re = pl.BlockSpec((LOCAL_WIN, SRC, 128), lambda b: (0, 0, b))
    spec_im = pl.BlockSpec((LOCAL_WIN, SRC, 128), lambda b: (0, 0, b + 4))
    rec_re = pl.BlockSpec((32, 128), lambda b: (0, b))
    rec_im = pl.BlockSpec((32, 128), lambda b: (0, b + 4))
    return pl.pallas_call(
        pack_kernel,
        grid=(4,),
        in_specs=[spec_re, spec_im, rec_re, rec_im],
        out_specs=pl.BlockSpec((8, 2, 144, 128), lambda b: (b, 0, 0, 0)),
        out_shape=jax.ShapeDtypeStruct((HOLDERS, 2, 144, 128), BF16),
        scratch_shapes=[pltpu.VMEM((2048, 128), F32), pltpu.VMEM((256, 128), F32)],
        compiler_params=params(),
    )(source_spectra, source_spectra, masked, masked)


def select_kernel(plan, block_ref, rec_ref, mine_ref, other_ref, spread):
    step = pl.program_id(0)
    core = plan[STEPS]

    @pl.when(step < STEPS)
    def _():
        mine_ref[0] = block_ref[0, core, :128, :]
        other_ref[0] = block_ref[0, 1 - core, :128, :]

    @pl.when(step == STEPS)
    def _():
        flat = rec_ref[...].reshape(HOLDERS * 32, 128)
        row = lax.broadcasted_iota(jnp.int32, (128, 128), 0)
        lane = lax.broadcasted_iota(jnp.int32, (128, 128), 1)
        holder = lax.broadcasted_iota(jnp.int32, (HOLDERS, 32, 128), 0)
        own = lax.broadcasted_iota(jnp.int32, (HOLDERS, 32, 128), 2) // 4 == holder
        for w in range(LOCAL_WIN):
            place = jnp.where(row == 4 * w + lane % 4, 1.0, 0.0).astype(BF16)
            tiled = jnp.dot(flat, place, preferred_element_type=F32).reshape(HOLDERS, 32, 128)
            spread[pl.ds(w, 32, stride=LOCAL_WIN), :] = jnp.sum(jnp.where(own, tiled, 0.0), axis=0)
        mine_ref[0] = spread[pl.ds(pl.multiple_of(core * 128, 128), 128), :].astype(BF16)
        other_ref[0] = spread[pl.ds(pl.multiple_of((1 - core) * 128, 128), 128), :].astype(BF16)


def select(plan, blocks):
    shape = jax.ShapeDtypeStruct((STEPS + 1, 128, 128), BF16)
    return pl.pallas_call(
        select_kernel,
        grid_spec=pltpu.PrefetchScalarGridSpec(
            num_scalar_prefetch=1,
            grid=(STEPS + 1,),
            in_specs=[
                pl.BlockSpec((1, 2, 144, 128), lambda s, plan: (plan[jnp.minimum(s, STEPS - 1)], 0, 0, 0)),
                pl.BlockSpec((HOLDERS, 2, 16, 128), lambda s, plan: (0, 0, 8, 0)),
            ],
            out_specs=[pl.BlockSpec((1, 128, 128), lambda s, plan: (s, 0, 0))] * 2,
            scratch_shapes=[pltpu.VMEM((256, 128), F32)],
        ),
        out_shape=[shape, shape],
        compiler_params=params(),
    )(plan, blocks, blocks)


def stack_kernel(a_ref, b_ref, c_ref, d_ref, out_ref, weights, tall):
    step = pl.program_id(0)
    groups = (a_ref, b_ref, c_ref, d_ref)

    @pl.when(step == 0)
    def _():
        for i in range(FINE):
            real, imag = [], []
            for ref in groups:
                tile = ref[STEPS, 16 * i : 16 * i + 16, :].astype(F32)
                real += [tile]
                imag += [-tile[8:], tile[:8]]
            both = jnp.concatenate([jnp.concatenate(real, axis=0), jnp.concatenate(imag, axis=0)], axis=1)
            weights[i] = both.T.astype(BF16)

    for i in range(FINE):
        block = jnp.concatenate([ref[step, 16 * i : 16 * i + 16, :] for ref in groups], axis=0)
        both = jnp.dot(weights[i], block, preferred_element_type=F32)
        tall[pl.ds(i, 128, stride=16), :] = both[:128]
        tall[pl.ds(FINE + i, 128, stride=16), :] = both[128:]
    out_ref[:, 0] = tall[...].reshape(HOLDERS, 64, 128).astype(BF16)


def stack(groups):
    whole = pl.BlockSpec((STEPS + 1, 128, 128), lambda s: (0, 0, 0))
    return pl.pallas_call(
        stack_kernel,
        grid=(STEPS,),
        in_specs=[whole] * 4,
        out_specs=pl.BlockSpec((HOLDERS, 1, 64, 128), lambda s: (0, s, 0, 0)),
        out_shape=jax.ShapeDtypeStruct((HOLDERS, STEPS, 64, 128), BF16),
        scratch_shapes=[pltpu.VMEM((FINE, 256, 64), BF16), pltpu.VMEM((2048, 128), F32)],
        compiler_params=params(),
    )(*groups)


def project_kernel(own_ref, far_ref, own_table, far_table, taper_ref, out_ref, tall):
    for r in range(4):
        rows = slice(16 * r, 16 * r + 16)
        own = own_ref[:, 0, rows, :].reshape(512, 128)
        far = far_ref[:, 0, rows, :].reshape(512, 128)
        dims = (((0,), (0,)), ((), ()))
        total = lax.dot_general(own, own_table[...], dims, preferred_element_type=F32)
        total += lax.dot_general(far, far_table[...], dims, preferred_element_type=F32)
        total = total * taper_ref[...]
        for b in range(0, total.shape[1], 128):
            tall[b // 128, pl.ds(r, 128, stride=4), :] = total[:, b : b + 128]
    for b in range(0, out_ref.shape[3], 128):
        out_ref[0, :, :, b : b + 128] = tall[b // 128].reshape(128, 4, 128).astype(BF16)


def project(own, far, own_table, far_table, taper):
    count = own_table.shape[1]
    block = pl.BlockSpec((HOLDERS, 1, 64, 128), lambda s: (0, s, 0, 0))
    table = pl.BlockSpec((512, count), lambda s: (0, 0))
    return pl.pallas_call(
        project_kernel,
        grid=(STEPS,),
        in_specs=[block, block, table, table, pl.BlockSpec((1, count), lambda s: (0, 0))],
        out_specs=pl.BlockSpec((1, SRC, 4, count), lambda s: (s, 0, 0, 0)),
        out_shape=jax.ShapeDtypeStruct((STEPS, SRC, 4, count), BF16),
        scratch_shapes=[pltpu.VMEM((count // 128, 512, 128), F32)],
        compiler_params=params(),
    )(own, far, own_table, far_table, taper)


def waves(wave, shift):
    angle = (wave[:, None] * shift[None, :] % (2 * LAGS)).astype(F32) * (math.pi / LAGS)
    return jnp.cos(angle), jnp.sin(angle)


def build_tables(start, count, core, scale):
    shift = jnp.arange(count, dtype=jnp.int32) + start - LAGS // 2
    fine_cos, fine_sin = waves(jnp.arange(FINE, dtype=jnp.int32), shift)
    tables = []
    for h in (core, 1 - core):
        coarse = 16 * jnp.arange(HOLDERS, dtype=jnp.int32) + FREQ // 8 + 8 * h
        cos, sin = waves(coarse, shift)
        cos, sin = cos[:, None, :] * scale, sin[:, None, :] * scale
        real = cos * fine_cos - sin * fine_sin
        imag = -(sin * fine_cos + cos * fine_sin)
        tables.append(jnp.stack([real, imag], axis=1).astype(BF16).reshape(512, count))
    return tables


def build_taper(start, count):
    position = jnp.arange(count, dtype=jnp.int32) + start
    edge = jnp.minimum(position, LAGS - 1 - position) + 1
    return jnp.minimum(1.0, edge.astype(F32) / (LAGS // 16))


def shards(source_spectra, receiver_spectra, quality_mask, owner_plan):
    win = lax.axis_index("win")
    core = win % 2
    count = LAGS // 4
    scale = 1.0 / math.sqrt(FREQ * LOCAL_WIN * 4)
    own_table, far_table = build_tables(win * count, count, core, scale)
    taper = build_taper(win * count, count)[None, :]
    masked = (receiver_spectra * quality_mask.astype(BF16)[:, :, None]).reshape(32, 2 * FREQ)
    packed = pack(source_spectra, masked)
    held = lax.all_to_all(packed, "chan", 0, 0, tiled=True)
    plan = jnp.concatenate([owner_plan, core[None].astype(jnp.int32)])
    mine, other = select(plan, held)
    from_core = lax.ppermute(other, "win", CORE_SWAP)
    from_half = lax.ppermute(mine, "win", HALF_SWAP)
    from_both = lax.ppermute(from_core, "win", HALF_SWAP)
    stacked = stack([mine, from_core, from_half, from_both])
    own = lax.all_to_all(stacked, "chan", 0, 0, tiled=True)
    far = lax.ppermute(own, "win", CORE_SWAP)
    return project(own, far, own_table, far_table, taper)


def solution(mesh):
    return jax.shard_map(
        shards,
        mesh=mesh,
        in_specs=(P("win", "chan", None), P("win", "chan", None), P("win", "chan"), P()),
        out_specs=P(None, None, "chan", "win"),
        check_vma=False,
    )
```

```python
import functools
import math

import jax
import jax.numpy as jnp
from jax import lax
from jax.experimental import pallas as pl
from jax.experimental.pallas import tpu as pltpu
from jax.sharding import PartitionSpec as P

LAGS = 4096
STEPS = 6
FREQ = 512
SRC = 128
HOLDERS = 32
PEERS = 64
LOCAL_WIN = 8
FINE = 4
ROWS = 144
F32 = jnp.float32
BF16 = jnp.bfloat16
CORE_SWAP = [(0, 1), (1, 0), (2, 3), (3, 2)]
SAME_CORE = [[(2 * half + core) * HOLDERS + c for half in range(2) for c in range(HOLDERS)] for core in range(2)]


def params(mebibytes):
    return pltpu.CompilerParams(vmem_limit_bytes=mebibytes * 1024 * 1024)


def pack_kernel(mask_ref, re_ref, im_ref, rec_re_ref, rec_im_ref, out_ref, tall, wide, small):
    for part, ref in enumerate((re_ref, im_ref)):
        for w in range(LOCAL_WIN):
            tall[pl.ds(part * LOCAL_WIN + w, 128, stride=16), :] = ref[w].astype(F32).T
    out_ref[:, :128, :] = tall[...].reshape(16, 128, 128).astype(BF16)
    lane = lax.broadcasted_iota(jnp.int32, (1, 128), 1)
    usable = jnp.zeros((1, 128), F32)
    for w in range(LOCAL_WIN):
        for r in range(4):
            usable = jnp.where(lane == 4 * w + r, mask_ref[r, w].astype(F32), usable)
    wide[32:, :] = jnp.zeros((96, 128), F32)
    for part, ref in enumerate((rec_re_ref, rec_im_ref)):
        for w in range(LOCAL_WIN):
            wide[4 * w : 4 * w + 4, :] = ref[w].astype(F32)
        small[pl.ds(part, 128, stride=2), :] = wide[...].T * usable
    out_ref[:, 128:, :] = small[...].reshape(16, 16, 128).astype(BF16)


def pack(source_spectra, receiver_spectra, quality_mask):
    spec_re = pl.BlockSpec((LOCAL_WIN, SRC, 128), lambda b: (0, 0, b))
    spec_im = pl.BlockSpec((LOCAL_WIN, SRC, 128), lambda b: (0, 0, b + 4))
    rec_re = pl.BlockSpec((LOCAL_WIN, 4, 128), lambda b: (0, 0, b))
    rec_im = pl.BlockSpec((LOCAL_WIN, 4, 128), lambda b: (0, 0, b + 4))
    return pl.pallas_call(
        pack_kernel,
        grid=(4,),
        in_specs=[pl.BlockSpec(memory_space=pltpu.SMEM), spec_re, spec_im, rec_re, rec_im],
        out_specs=pl.BlockSpec((16, ROWS, 128), lambda b: (b, 0, 0)),
        out_shape=jax.ShapeDtypeStruct((PEERS, ROWS, 128), BF16),
        scratch_shapes=[pltpu.VMEM((2048, 128), F32), pltpu.VMEM((128, 128), F32), pltpu.VMEM((256, 128), F32)],
        compiler_params=params(60),
    )(quality_mask.T, source_spectra, source_spectra, receiver_spectra, receiver_spectra)


def select_kernel(plan, held_ref, mine_ref, other_ref, spread):
    core = lax.axis_index("win") % 2
    own = pl.ds(pl.multiple_of(64 * core, 64), 64)
    far = pl.ds(pl.multiple_of(64 * (1 - core), 64), 64)
    flat = held_ref[:, :, 128:, :].reshape(PEERS * 16, 128)
    row = lax.broadcasted_iota(jnp.int32, (128, 128), 0)
    lane = lax.broadcasted_iota(jnp.int32, (128, 128), 1)
    holder = lax.broadcasted_iota(jnp.int32, (HOLDERS, 16, 128), 0)
    here = lax.broadcasted_iota(jnp.int32, (HOLDERS, 16, 128), 2) // 4 == holder
    for w in range(LOCAL_WIN):
        place = jnp.where(row == 4 * w + lane % 4, 1.0, 0.0).astype(BF16)
        tiled = jnp.dot(flat, place, preferred_element_type=F32).reshape(2, HOLDERS, 16, 128)
        for half in range(2):
            one = jnp.sum(jnp.where(here, tiled[half], 0.0), axis=0)
            spread[half, pl.ds(w, 16, stride=LOCAL_WIN), :] = one
    for half in range(2):
        to = slice(64 * half, 64 * half + 64)
        mine_ref[0, to, :] = spread[half, own, :].astype(BF16)
        other_ref[0, to, :] = spread[half, far, :].astype(BF16)
        for step in range(STEPS):
            mine_ref[step + 1, to, :] = held_ref[half, plan[step], own, :]
            other_ref[step + 1, to, :] = held_ref[half, plan[step], far, :]


def select(plan, blocks):
    return pl.pallas_call(
        select_kernel,
        in_specs=[pl.BlockSpec(memory_space=pltpu.SMEM), pl.BlockSpec(memory_space=pltpu.VMEM)],
        out_shape=[jax.ShapeDtypeStruct((STEPS + 1, 128, 128), BF16)] * 2,
        scratch_shapes=[pltpu.VMEM((2, 128, 128), F32)],
        compiler_params=params(16),
    )(plan, blocks)


def stack_kernel(a, b, out_ref, weights, tall):
    def tiles(step, i):
        return [ref[step, 64 * half + 16 * i : 64 * half + 16 * i + 16, :] for ref in (a, b) for half in range(2)]

    for i in range(FINE):
        real, imag = [], []
        for tile in tiles(0, i):
            tile = tile.astype(F32)
            real += [tile]
            imag += [-tile[8:], tile[:8]]
        both = jnp.concatenate([jnp.concatenate(real, axis=0), jnp.concatenate(imag, axis=0)], axis=1)
        weights[i] = both.T.astype(BF16)

    @pl.loop(0, STEPS)
    def _(step):
        for i in range(FINE):
            block = jnp.concatenate(tiles(step + 1, i), axis=0)
            both = jnp.dot(weights[i], block, preferred_element_type=F32)
            tall[pl.ds(i, 128, stride=8), :] = both[:128]
            tall[pl.ds(FINE + i, 128, stride=8), :] = both[128:]
        spectra = tall[...].reshape(HOLDERS, 32, 128).astype(BF16)
        for half in range(2):
            out_ref[half, :, step] = spectra


def stack(mine, from_core):
    return pl.pallas_call(
        stack_kernel,
        out_shape=jax.ShapeDtypeStruct((2, HOLDERS, STEPS, 32, 128), BF16),
        scratch_shapes=[pltpu.VMEM((FINE, 256, 64), BF16), pltpu.VMEM((1024, 128), F32)],
        compiler_params=params(16),
    )(mine, from_core).reshape(PEERS, STEPS, 32, 128)


def wide(ref, step):
    held = ref[:, step].astype(F32)
    return jnp.concatenate([held[:, 8 * r : 8 * r + 8, :].reshape(512, 128) for r in range(4)], axis=1).astype(BF16)


def turn(block, table):
    return lax.dot_general(block, table, (((0,), (0,)), ((), ())), preferred_element_type=F32)


def begin_kernel(own_ref, table_ref, out_ref):
    @pl.loop(0, STEPS)
    def _(step):
        out_ref[step] = turn(wide(own_ref, step), table_ref[...])


def begin(own, table):
    count = table.shape[1]
    return pl.pallas_call(
        begin_kernel,
        out_shape=jax.ShapeDtypeStruct((STEPS, 512, count), F32),
        compiler_params=params(8),
        cost_estimate=pl.CostEstimate(flops=STEPS * 1_000_000_000, bytes_accessed=16_000_000, transcendentals=0),
    )(own, table)


def finish_kernel(part_ref, far_ref, table_ref, taper_ref, out_ref, tall, ready, sems):
    count = table_ref.shape[1]

    def send(step, slot):
        return pltpu.make_async_copy(ready.at[slot], out_ref.at[step], sems.at[slot])

    @pl.loop(0, STEPS)
    def _(step):
        slot = lax.rem(step, 2)
        total = (turn(wide(far_ref, step), table_ref[...]) + part_ref[step]) * taper_ref[...]
        for r in range(4):
            for b in range(0, count, 128):
                tall[b // 128, pl.ds(r, 128, stride=4), :] = total[128 * r : 128 * r + 128, b : b + 128]

        @pl.when(step >= 2)
        def _():
            send(step - 2, slot).wait()

        for b in range(0, count, 128):
            ready[slot, :, :, b : b + 128] = tall[b // 128].reshape(128, 4, 128).astype(BF16)
        send(step, slot).start()

    send(STEPS - 2, 0).wait()
    send(STEPS - 1, 1).wait()


def finish(part, far, table, taper):
    count = table.shape[1]
    return pl.pallas_call(
        finish_kernel,
        out_specs=pl.BlockSpec(memory_space=pl.ANY),
        out_shape=jax.ShapeDtypeStruct((STEPS, SRC, 4, count), BF16),
        scratch_shapes=[
            pltpu.VMEM((count // 128, 512, 128), F32),
            pltpu.VMEM((2, SRC, 4, count), BF16),
            pltpu.SemaphoreType.DMA((2,)),
        ],
        compiler_params=params(16),
        cost_estimate=pl.CostEstimate(flops=STEPS * 1_000_000_000, bytes_accessed=22_000_000, transcendentals=0),
    )(part, far, table, taper)


def table_kernel(win_ref, own_ref, far_ref, taper_ref, *, count, scale):
    start = win_ref[0] * count
    core = win_ref[0] % 2
    shift = lax.broadcasted_iota(jnp.int32, (8, count), 1) + (start - LAGS // 2)
    index = lax.broadcasted_iota(jnp.int32, (8, count), 0)

    def waves(wave):
        angle = ((wave * shift) & (2 * LAGS - 1)).astype(F32) * (math.pi / LAGS)
        return jnp.cos(angle), jnp.sin(angle)

    high_cos, high_sin = waves(64 * index + 64)
    mid_cos, mid_sin = waves(8 * index)
    low_cos, low_sin = waves(index)
    high_cos, high_sin = high_cos * scale, high_sin * scale
    for ref, h in ((own_ref, core), (far_ref, 1 - core)):
        def rows(wave):
            return jnp.where(h == 0, jnp.concatenate([wave[:4]] * 2, axis=0), jnp.concatenate([wave[4:]] * 2, axis=0))

        fine_cos, fine_sin = rows(low_cos), rows(low_sin)
        real = index < 4
        by_cos = jnp.where(real, fine_cos, -fine_sin)
        by_sin = jnp.where(real, -fine_sin, -fine_cos)
        for a in range(8):
            for b in range(8):
                cos = high_cos[a : a + 1] * mid_cos[b : b + 1] - high_sin[a : a + 1] * mid_sin[b : b + 1]
                sin = high_sin[a : a + 1] * mid_cos[b : b + 1] + high_cos[a : a + 1] * mid_sin[b : b + 1]
                ref[8 * (8 * a + b) : 8 * (8 * a + b) + 8, :] = (cos * by_cos + sin * by_sin).astype(BF16)
    position = lax.broadcasted_iota(jnp.int32, (1, count), 1) + start
    edge = jnp.minimum(position, LAGS - 1 - position) + 1
    taper_ref[...] = jnp.minimum(1.0, edge.astype(F32) / (LAGS // 16))


def build_tables(win, count, scale):
    table = jax.ShapeDtypeStruct((512, count), BF16)
    return pl.pallas_call(
        functools.partial(table_kernel, count=count, scale=scale),
        in_specs=[pl.BlockSpec(memory_space=pltpu.SMEM)],
        out_shape=[table, table, jax.ShapeDtypeStruct((1, count), F32)],
        compiler_params=params(8),
    )(win)


def shards(source_spectra, receiver_spectra, quality_mask, owner_plan):
    count = LAGS // 4
    scale = 1.0 / math.sqrt(FREQ * LOCAL_WIN * 4)
    packed = pack(source_spectra, receiver_spectra, quality_mask)
    held = exchange(packed).reshape(2, HOLDERS, ROWS, 128)
    mine, other = select(owner_plan, held)
    from_core = lax.ppermute(other, "win", CORE_SWAP)
    win, mine = lax.optimization_barrier((lax.axis_index("win")[None], mine))
    own_table, far_table, taper = build_tables(win, count, scale)
    mine, own_table = lax.optimization_barrier((mine, own_table))
    own = exchange(stack(mine, from_core))
    far = lax.ppermute(own, "win", CORE_SWAP)
    return finish(begin(own, own_table), far, far_table, taper)


def exchange(blocks):
    return lax.all_to_all(blocks, ("win", "chan"), 0, 0, tiled=True, axis_index_groups=SAME_CORE)


def solution(mesh):
    return jax.shard_map(
        shards,
        mesh=mesh,
        in_specs=(P("win", "chan", None), P("win", "chan", None), P("win", "chan"), P()),
        out_specs=P(None, None, "chan", "win"),
        check_vma=False,
    )
```

```python
import functools
import math

import jax
import jax.numpy as jnp
from jax import lax
from jax.experimental import pallas as pl
from jax.experimental.pallas import tpu as pltpu
from jax.sharding import PartitionSpec as P

LAGS = 4096
STEPS = 6
FREQ = 512
SRC = 128
HOLDERS = 32
PEERS = 64
LOCAL_WIN = 8
FINE = 4
ROWS = 136
F32 = jnp.float32
BF16 = jnp.bfloat16
CORE_SWAP = [(0, 1), (1, 0), (2, 3), (3, 2)]
SAME_CORE = [[(2 * half + core) * HOLDERS + c for half in range(2) for c in range(HOLDERS)] for core in range(2)]


def params(mebibytes):
    return pltpu.CompilerParams(vmem_limit_bytes=mebibytes * 1024 * 1024)


def pack_kernel(mask_ref, re_ref, im_ref, rec_re_ref, rec_im_ref, out_ref, block):
    lane = lax.broadcasted_iota(jnp.int32, (1, 128), 1)
    usable = jnp.zeros((1, 128), F32)
    for w in range(LOCAL_WIN):
        for r in range(4):
            usable = jnp.where(lane % 32 == 4 * w + r, mask_ref[r, w].astype(F32), usable)
    block[64:, :] = jnp.zeros((64, 128), F32)
    for b in range(2):
        lanes = slice(128 * b, 128 * b + 128)
        peers = slice(16 * b, 16 * b + 16)
        for part, ref in enumerate((rec_re_ref, rec_im_ref)):
            for w in range(LOCAL_WIN):
                row = 32 * part + 4 * w
                block[row : row + 4, :] = ref[w, :, lanes].astype(F32)
        out_ref[peers, 128:, :] = (block[...].T * usable).reshape(16, 8, 128).astype(BF16)
        for part, ref in enumerate((re_ref, im_ref)):
            for w in range(0, LOCAL_WIN, 2):
                pair = [ref[w + k, :, lanes].astype(F32).T.reshape(16, 8, 128) for k in range(2)]
                row = 64 * part + 8 * w
                out_ref[peers, row : row + 16, :] = jnp.concatenate(pair, axis=1).astype(BF16)


def pack(source_spectra, receiver_spectra, quality_mask):
    return pl.pallas_call(
        pack_kernel,
        grid=(2,),
        in_specs=[
            pl.BlockSpec(memory_space=pltpu.SMEM),
            pl.BlockSpec((LOCAL_WIN, SRC, 256), lambda b: (0, 0, b)),
            pl.BlockSpec((LOCAL_WIN, SRC, 256), lambda b: (0, 0, b + 2)),
            pl.BlockSpec((LOCAL_WIN, 4, 256), lambda b: (0, 0, b)),
            pl.BlockSpec((LOCAL_WIN, 4, 256), lambda b: (0, 0, b + 2)),
        ],
        out_specs=pl.BlockSpec((32, ROWS, 128), lambda b: (b, 0, 0)),
        out_shape=jax.ShapeDtypeStruct((PEERS, ROWS, 128), BF16),
        scratch_shapes=[pltpu.VMEM((128, 128), F32)],
        compiler_params=params(60),
    )(quality_mask.T, source_spectra, source_spectra, receiver_spectra, receiver_spectra)


def select_kernel(plan, held_ref, mine_ref, other_ref, spread, chosen):
    core = lax.axis_index("win") % 2
    own = pl.ds(pl.multiple_of(64 * core, 64), 64)
    far = pl.ds(pl.multiple_of(64 * (1 - core), 64), 64)
    flat = held_ref[:, :, 128:, :].reshape(PEERS * 8, 128)
    row = lax.broadcasted_iota(jnp.int32, (128, 128), 0)
    lane = lax.broadcasted_iota(jnp.int32, (128, 128), 1)
    holder = lax.broadcasted_iota(jnp.int32, (HOLDERS, 8, 128), 0)
    here = lax.broadcasted_iota(jnp.int32, (HOLDERS, 8, 128), 2) // 4 == holder
    for k in range(2 * LOCAL_WIN):
        place = jnp.where(row == 4 * k + lane % 4, 1.0, 0.0).astype(BF16)
        tiled = jnp.dot(flat, place, preferred_element_type=F32).reshape(2, HOLDERS, 8, 128)
        for half in range(2):
            spread[half, pl.ds(k, 8, stride=16), :] = jnp.sum(jnp.where(here, tiled[half], 0.0), axis=0)
    for half in range(2):
        to = slice(64 * half, 64 * half + 64)
        mine_ref[0, to, :] = spread[half, own, :].astype(BF16)
        other_ref[0, to, :] = spread[half, far, :].astype(BF16)
        for step in range(STEPS):
            chosen[half, step] = held_ref[half, plan[step], :128, :].astype(F32)
            for i in range(FINE):
                to = slice(64 * half + 16 * i, 64 * half + 16 * i + 16)
                mine_ref[step + 1, to, :] = chosen[half, step, pl.ds(4 * core + i, 16, stride=8), :].astype(BF16)
                other_ref[step + 1, to, :] = chosen[half, step, pl.ds(4 * (1 - core) + i, 16, stride=8), :].astype(BF16)


def select(plan, blocks):
    return pl.pallas_call(
        select_kernel,
        in_specs=[pl.BlockSpec(memory_space=pltpu.SMEM), pl.BlockSpec(memory_space=pltpu.VMEM)],
        out_shape=[jax.ShapeDtypeStruct((STEPS + 1, 128, 128), BF16)] * 2,
        scratch_shapes=[pltpu.VMEM((2, 128, 128), F32), pltpu.VMEM((2, STEPS, 128, 128), F32)],
        compiler_params=params(16),
    )(plan, blocks)


def stack_kernel(a, b, out_ref, weights, tall):
    def tiles(step, i):
        return [ref[step, 64 * half + 16 * i : 64 * half + 16 * i + 16, :] for ref in (a, b) for half in range(2)]

    for i in range(FINE):
        real, imag = [], []
        for tile in tiles(0, i):
            tile = tile.astype(F32)
            real += [tile]
            imag += [-tile[8:], tile[:8]]
        both = jnp.concatenate([jnp.concatenate(real, axis=0), jnp.concatenate(imag, axis=0)], axis=1)
        weights[i] = both.T.astype(BF16)

    @pl.loop(0, STEPS, step=2)
    def _(step):
        for i in range(FINE):
            pair = [jnp.concatenate(tiles(step + 1 + k, i), axis=0) for k in range(2)]
            both = jnp.dot(weights[i], jnp.concatenate(pair, axis=1), preferred_element_type=F32)
            for k in range(2):
                tall[k, pl.ds(i, 128, stride=8), :] = both[:128, 128 * k : 128 * k + 128]
                tall[k, pl.ds(FINE + i, 128, stride=8), :] = both[128:, 128 * k : 128 * k + 128]
        for k in range(2):
            spectra = tall[k].reshape(HOLDERS, 32, 128).astype(BF16)
            for half in range(2):
                out_ref[half, :, step + k] = spectra


def stack(mine, from_core):
    return pl.pallas_call(
        stack_kernel,
        out_shape=jax.ShapeDtypeStruct((2, HOLDERS, STEPS, 32, 128), BF16),
        scratch_shapes=[pltpu.VMEM((FINE, 256, 64), BF16), pltpu.VMEM((2, 1024, 128), F32)],
        compiler_params=params(16),
    )(mine, from_core).reshape(PEERS, STEPS, 32, 128)


def arrange(ref, step, lhs):
    held = ref[:, step].astype(F32)
    for r in range(4):
        turned = held[:, 8 * r : 8 * r + 8, :].reshape(512, 128).T
        for b in range(4):
            lhs[b, pl.ds(r, 128, stride=4), :] = turned[:, 128 * b : 128 * b + 128]


def rows(lhs):
    return jnp.concatenate([lhs[b].astype(BF16) for b in range(4)], axis=1)


def begin_kernel(own_ref, table_ref, out_ref, lhs):
    @pl.loop(0, STEPS)
    def _(step):
        arrange(own_ref, step, lhs)
        out_ref[step] = jnp.dot(rows(lhs), table_ref[...], preferred_element_type=F32)


def begin(own, table):
    count = table.shape[1]
    return pl.pallas_call(
        begin_kernel,
        out_shape=jax.ShapeDtypeStruct((STEPS, 512, count), F32),
        scratch_shapes=[pltpu.VMEM((4, 512, 128), F32)],
        compiler_params=params(8),
        cost_estimate=pl.CostEstimate(flops=STEPS * 1_000_000_000, bytes_accessed=16_000_000, transcendentals=0),
    )(own, table)


def finish_kernel(part_ref, far_ref, table_ref, taper_ref, out_ref, even, odd, ready, sems):
    count = table_ref.shape[1]
    lhs = (even, odd)

    def send(step, slot):
        return pltpu.make_async_copy(ready.at[slot], out_ref.at[step], sems.at[slot])

    arrange(far_ref, 0, even)

    @pl.loop(0, STEPS, step=2)
    def _(first):
        for slot in range(2):
            step = first + slot
            block = rows(lhs[slot])

            @pl.when(step >= 2)
            def _():
                send(step - 2, slot).wait()

            for n in range(0, count, 256):
                lags = slice(n, n + 256)
                total = jnp.dot(block, table_ref[:, lags], preferred_element_type=F32) + part_ref[step, :, lags]
                ready[slot, :, :, lags] = (total * taper_ref[:, lags]).reshape(SRC, 4, 256).astype(BF16)
            arrange(far_ref, jnp.minimum(step + 1, STEPS - 1), lhs[1 - slot])
            send(step, slot).start()

    send(STEPS - 2, 0).wait()
    send(STEPS - 1, 1).wait()


def finish(part, far, table, taper):
    count = table.shape[1]
    return pl.pallas_call(
        finish_kernel,
        out_specs=pl.BlockSpec(memory_space=pl.ANY),
        out_shape=jax.ShapeDtypeStruct((STEPS, SRC, 4, count), BF16),
        scratch_shapes=[
            pltpu.VMEM((4, 512, 128), F32),
            pltpu.VMEM((4, 512, 128), F32),
            pltpu.VMEM((2, SRC, 4, count), BF16),
            pltpu.SemaphoreType.DMA((2,)),
        ],
        compiler_params=params(16),
        cost_estimate=pl.CostEstimate(flops=STEPS * 1_000_000_000, bytes_accessed=22_000_000, transcendentals=0),
    )(part, far, table, taper)


def table_kernel(win_ref, own_ref, far_ref, taper_ref, *, count, scale):
    start = win_ref[0] * count
    core = win_ref[0] % 2
    shift = lax.broadcasted_iota(jnp.int32, (8, count), 1) + (start - LAGS // 2)
    index = lax.broadcasted_iota(jnp.int32, (8, count), 0)

    def waves(wave):
        angle = ((wave * shift) & (2 * LAGS - 1)).astype(F32) * (math.pi / LAGS)
        return jnp.cos(angle), jnp.sin(angle)

    high_cos, high_sin = waves(64 * index + 64)
    mid_cos, mid_sin = waves(8 * index)
    low_cos, low_sin = waves(index)
    high_cos, high_sin = high_cos * scale, high_sin * scale
    for ref, h in ((own_ref, core), (far_ref, 1 - core)):
        def rows(wave):
            return jnp.where(h == 0, jnp.concatenate([wave[:4]] * 2, axis=0), jnp.concatenate([wave[4:]] * 2, axis=0))

        fine_cos, fine_sin = rows(low_cos), rows(low_sin)
        real = index < 4
        by_cos = jnp.where(real, fine_cos, -fine_sin)
        by_sin = jnp.where(real, -fine_sin, -fine_cos)
        for a in range(8):
            for b in range(8):
                cos = high_cos[a : a + 1] * mid_cos[b : b + 1] - high_sin[a : a + 1] * mid_sin[b : b + 1]
                sin = high_sin[a : a + 1] * mid_cos[b : b + 1] + high_cos[a : a + 1] * mid_sin[b : b + 1]
                ref[8 * (8 * a + b) : 8 * (8 * a + b) + 8, :] = (cos * by_cos + sin * by_sin).astype(BF16)
    position = lax.broadcasted_iota(jnp.int32, (1, count), 1) + start
    edge = jnp.minimum(position, LAGS - 1 - position) + 1
    taper_ref[...] = jnp.minimum(1.0, edge.astype(F32) / (LAGS // 16))


def build_tables(win, count, scale):
    table = jax.ShapeDtypeStruct((512, count), BF16)
    return pl.pallas_call(
        functools.partial(table_kernel, count=count, scale=scale),
        in_specs=[pl.BlockSpec(memory_space=pltpu.SMEM)],
        out_shape=[table, table, jax.ShapeDtypeStruct((1, count), F32)],
        compiler_params=params(8),
    )(win)


def shards(source_spectra, receiver_spectra, quality_mask, owner_plan):
    count = LAGS // 4
    scale = 1.0 / math.sqrt(FREQ * LOCAL_WIN * 4)
    packed = pack(source_spectra, receiver_spectra, quality_mask)
    held = exchange(packed).reshape(2, HOLDERS, ROWS, 128)
    mine, other = select(owner_plan, held)
    from_core = lax.ppermute(other, "win", CORE_SWAP)
    win, mine = lax.optimization_barrier((lax.axis_index("win")[None], mine))
    own_table, far_table, taper = build_tables(win, count, scale)
    mine, own_table = lax.optimization_barrier((mine, own_table))
    own = exchange(stack(mine, from_core))
    far = lax.ppermute(own, "win", CORE_SWAP)
    return finish(begin(own, own_table), far, far_table, taper)


def exchange(blocks):
    return lax.all_to_all(blocks, ("win", "chan"), 0, 0, tiled=True, axis_index_groups=SAME_CORE)


def solution(mesh):
    return jax.shard_map(
        shards,
        mesh=mesh,
        in_specs=(P("win", "chan", None), P("win", "chan", None), P("win", "chan"), P()),
        out_specs=P(None, None, "chan", "win"),
        check_vma=False,
    )
```

```python
import math

import jax
import jax.numpy as jnp
from jax import lax
from jax.experimental import pallas as pl
from jax.experimental.pallas import tpu as pltpu
from jax.sharding import PartitionSpec as P

LAGS = 4096
STEPS = 6
FREQ = 512
SRC = 128
HOLDERS = 32
PEERS = 64
LOCAL_WIN = 8
FINE = 4
ROWS = 72
GROUPS = 4
F32 = jnp.float32
BF16 = jnp.bfloat16
CORE_SWAP = [(0, 1), (1, 0), (2, 3), (3, 2)]
SAME_CORE = [[(2 * half + core) * HOLDERS + c for half in range(2) for c in range(HOLDERS)] for core in range(2)]


def params(mebibytes):
    return pltpu.CompilerParams(vmem_limit_bytes=mebibytes * 1024 * 1024)


def pack_kernel(mask_ref, re_ref, im_ref, rec_re_ref, rec_im_ref, out_ref, block):
    lane = lax.broadcasted_iota(jnp.int32, (1, 128), 1)
    usable = jnp.zeros((1, 128), F32)
    for w in range(LOCAL_WIN):
        for r in range(4):
            usable = jnp.where(lane % 32 == 4 * w + r, mask_ref[r, w].astype(F32), usable)
    block[64:, :] = jnp.zeros((64, 128), F32)
    low = lax.broadcasted_iota(jnp.int32, (128, 128), 0) % 8 < 4

    def up(tiles):
        return pltpu.roll(tiles.reshape(128, 128), 124, 0)

    def down(tiles):
        return pltpu.roll(tiles.reshape(128, 128), 4, 0)

    for b in range(2):
        lanes = slice(128 * b, 128 * b + 128)
        for part, ref in enumerate((rec_re_ref, rec_im_ref)):
            for w in range(LOCAL_WIN):
                row = 32 * part + 4 * w
                block[row : row + 4, :] = ref[w, :, lanes].astype(F32)
        turned = block[...].T * usable
        for core, tiles in enumerate((turned, up(turned))):
            out_ref[32 * core + 16 * b : 32 * core + 16 * b + 16, 64:, :] = tiles.reshape(16, 8, 128).astype(BF16)
        for part, ref in enumerate((re_ref, im_ref)):
            for w in range(0, LOCAL_WIN, 4):
                first, second, third, fourth = (ref[w + k, :, lanes].astype(F32).T for k in range(4))
                cores = (
                    (jnp.where(low, first, down(second)), jnp.where(low, third, down(fourth))),
                    (jnp.where(low, up(first), second), jnp.where(low, up(third), fourth)),
                )
                row = 32 * part + 4 * w
                for core, pair in enumerate(cores):
                    both = jnp.concatenate([tiles.reshape(16, 8, 128) for tiles in pair], axis=1)
                    out_ref[32 * core + 16 * b : 32 * core + 16 * b + 16, row : row + 16, :] = both.astype(BF16)


def pack(source_spectra, receiver_spectra, quality_mask):
    return pl.pallas_call(
        pack_kernel,
        grid=(2,),
        in_specs=[
            pl.BlockSpec(memory_space=pltpu.SMEM),
            pl.BlockSpec((LOCAL_WIN, SRC, 256), lambda b: (0, 0, b)),
            pl.BlockSpec((LOCAL_WIN, SRC, 256), lambda b: (0, 0, b + 2)),
            pl.BlockSpec((LOCAL_WIN, 4, 256), lambda b: (0, 0, b)),
            pl.BlockSpec((LOCAL_WIN, 4, 256), lambda b: (0, 0, b + 2)),
        ],
        out_specs=pl.BlockSpec((64, ROWS, 128), lambda b: (b, 0, 0)),
        out_shape=jax.ShapeDtypeStruct((GROUPS * HOLDERS, ROWS, 128), BF16),
        scratch_shapes=[pltpu.VMEM((128, 128), F32)],
        compiler_params=params(60),
    )(quality_mask.T, source_spectra, source_spectra, receiver_spectra, receiver_spectra)


def stack_kernel(plan, held_ref, out_ref, spread, chosen, weights, tall):
    flat = held_ref[:, :, 64:, :].reshape(GROUPS * HOLDERS * 8, 128)
    row = lax.broadcasted_iota(jnp.int32, (128, 128), 0)
    lane = lax.broadcasted_iota(jnp.int32, (128, 128), 1)
    holder = lax.broadcasted_iota(jnp.int32, (HOLDERS, 8, 128), 0)
    here = lax.broadcasted_iota(jnp.int32, (HOLDERS, 8, 128), 2) // 4 == holder
    for k in range(2 * LOCAL_WIN):
        place = jnp.where(row == 4 * k + lane % 4, 1.0, 0.0).astype(BF16)
        tiled = jnp.dot(flat, place, preferred_element_type=F32).reshape(GROUPS, HOLDERS, 8, 128)
        for group in range(GROUPS):
            one = jnp.sum(jnp.where(here, tiled[group], 0.0), axis=0)
            spread[group, pl.ds(k, FINE, stride=16), :] = one[:FINE]
    for i in range(FINE):
        real, imag = [], []
        for group in range(GROUPS):
            tile = spread[group, 16 * i : 16 * i + 16, :]
            real += [tile]
            imag += [-tile[8:], tile[:8]]
        both = jnp.concatenate([jnp.concatenate(real, axis=0), jnp.concatenate(imag, axis=0)], axis=1)
        weights[i] = both.T.astype(BF16)

    @pl.loop(0, STEPS, step=2)
    def _(step):
        for k in range(2):
            for group in range(GROUPS):
                chosen[k, group] = held_ref[group, plan[step + k], :64, :].astype(F32)
        for i in range(FINE):
            pair = [
                jnp.concatenate([chosen[k, group, pl.ds(i, 16, stride=FINE), :] for group in range(GROUPS)], axis=0)
                for k in range(2)
            ]
            block = jnp.concatenate(pair, axis=1).astype(BF16)
            both = jnp.dot(weights[i], block, preferred_element_type=F32)
            for k in range(2):
                tall[k, pl.ds(i, 128, stride=8), :] = both[:128, 128 * k : 128 * k + 128]
                tall[k, pl.ds(FINE + i, 128, stride=8), :] = both[128:, 128 * k : 128 * k + 128]
        for k in range(2):
            spectra = tall[k].reshape(HOLDERS, 32, 128).astype(BF16)
            for half in range(2):
                out_ref[half, :, step + k] = spectra


def stack(plan, held):
    return pl.pallas_call(
        stack_kernel,
        in_specs=[pl.BlockSpec(memory_space=pltpu.SMEM), pl.BlockSpec(memory_space=pltpu.VMEM)],
        out_shape=jax.ShapeDtypeStruct((2, HOLDERS, STEPS, 32, 128), BF16),
        scratch_shapes=[
            pltpu.VMEM((GROUPS, 64, 128), F32),
            pltpu.VMEM((2, GROUPS, 64, 128), F32),
            pltpu.VMEM((FINE, 256, 64), BF16),
            pltpu.VMEM((2, 1024, 128), F32),
        ],
        compiler_params=params(8),
    )(plan, held).reshape(PEERS, STEPS, 32, 128)


def arrange(ref, step, lhs):
    held = ref[:, step].astype(F32)
    for r in range(4):
        turned = held[:, 8 * r : 8 * r + 8, :].reshape(512, 128).T
        for b in range(4):
            lhs[b, pl.ds(r, 128, stride=4), :] = turned[:, 128 * b : 128 * b + 128]


def rows(lhs):
    return jnp.concatenate([lhs[b].astype(BF16) for b in range(4)], axis=1)


def fill_tables(own_ref, far_ref, taper_ref):
    count = taper_ref.shape[1]
    scale = 1.0 / math.sqrt(FREQ * LOCAL_WIN * GROUPS)
    start = lax.axis_index("win") * count
    core = lax.axis_index("win") % 2
    shift = lax.broadcasted_iota(jnp.int32, (8, count), 1) + (start - LAGS // 2)
    index = lax.broadcasted_iota(jnp.int32, (8, count), 0)

    def waves(wave):
        angle = ((wave * shift) & (2 * LAGS - 1)).astype(F32) * (math.pi / LAGS)
        return jnp.cos(angle), jnp.sin(angle)

    high_cos, high_sin = waves(64 * index + 64)
    mid_cos, mid_sin = waves(8 * index)
    low_cos, low_sin = waves(index)
    high_cos, high_sin = high_cos * scale, high_sin * scale
    for ref, h in ((own_ref, core), (far_ref, 1 - core)):
        def rows(wave):
            return jnp.where(h == 0, jnp.concatenate([wave[:4]] * 2, axis=0), jnp.concatenate([wave[4:]] * 2, axis=0))

        fine_cos, fine_sin = rows(low_cos), rows(low_sin)
        real = index < 4
        by_cos = jnp.where(real, fine_cos, -fine_sin)
        by_sin = jnp.where(real, -fine_sin, -fine_cos)
        for a in range(8):
            for b in range(8):
                cos = high_cos[a : a + 1] * mid_cos[b : b + 1] - high_sin[a : a + 1] * mid_sin[b : b + 1]
                sin = high_sin[a : a + 1] * mid_cos[b : b + 1] + high_cos[a : a + 1] * mid_sin[b : b + 1]
                ref[8 * (8 * a + b) : 8 * (8 * a + b) + 8, :] = (cos * by_cos + sin * by_sin).astype(BF16)
    position = lax.broadcasted_iota(jnp.int32, (1, count), 1) + start
    edge = jnp.minimum(position, LAGS - 1 - position) + 1
    taper_ref[...] = jnp.minimum(1.0, edge.astype(F32) / (LAGS // 16))


def begin_kernel(own_ref, out_ref, far_table, taper_ref, own_table, lhs):
    fill_tables(own_table, far_table, taper_ref)

    @pl.loop(0, STEPS)
    def _(step):
        arrange(own_ref, step, lhs)
        out_ref[step] = jnp.dot(rows(lhs), own_table[...], preferred_element_type=F32)


def begin(own, count):
    return pl.pallas_call(
        begin_kernel,
        out_shape=[
            jax.ShapeDtypeStruct((STEPS, 512, count), F32),
            jax.ShapeDtypeStruct((512, count), BF16),
            jax.ShapeDtypeStruct((1, count), F32),
        ],
        scratch_shapes=[pltpu.VMEM((512, count), BF16), pltpu.VMEM((4, 512, 128), F32)],
        compiler_params=params(8),
        cost_estimate=pl.CostEstimate(flops=STEPS * 1_000_000_000, bytes_accessed=16_000_000, transcendentals=0),
    )(own)


def finish_kernel(part_ref, far_ref, table_ref, taper_ref, out_ref, even, odd, ready, sems):
    count = table_ref.shape[1]
    lhs = (even, odd)

    def send(step, piece):
        sources = pl.ds(64 * piece, 64)
        return pltpu.make_async_copy(ready.at[step, sources], out_ref.at[step, sources], sems.at[step, piece])

    arrange(far_ref, 0, even)
    for step in range(STEPS):
        block = rows(lhs[step % 2])
        for piece in range(2):
            here = slice(256 * piece, 256 * piece + 256)
            for n in range(0, count, 256):
                lags = slice(n, n + 256)
                total = jnp.dot(block[here], table_ref[:, lags], preferred_element_type=F32)
                total = (total + part_ref[step, here, lags]) * taper_ref[:, lags]
                ready[step, 64 * piece : 64 * piece + 64, :, lags] = total.reshape(64, 4, 256).astype(BF16)
            send(step, piece).start()
        if step + 1 < STEPS:
            arrange(far_ref, step + 1, lhs[1 - step % 2])
    for step in range(STEPS):
        for piece in range(2):
            send(step, piece).wait()


def finish(part, far, table, taper):
    count = table.shape[1]
    return pl.pallas_call(
        finish_kernel,
        out_specs=pl.BlockSpec(memory_space=pl.ANY),
        out_shape=jax.ShapeDtypeStruct((STEPS, SRC, 4, count), BF16),
        scratch_shapes=[
            pltpu.VMEM((4, 512, 128), F32),
            pltpu.VMEM((4, 512, 128), F32),
            pltpu.VMEM((STEPS, SRC, 4, count), BF16),
            pltpu.SemaphoreType.DMA((STEPS, 2)),
        ],
        compiler_params=params(24),
        cost_estimate=pl.CostEstimate(flops=STEPS * 1_000_000_000, bytes_accessed=22_000_000, transcendentals=0),
    )(part, far, table, taper)


def shards(source_spectra, receiver_spectra, quality_mask, owner_plan):
    packed = pack(source_spectra, receiver_spectra, quality_mask)
    held = lax.all_to_all(packed, ("win", "chan"), 0, 0, tiled=True).reshape(GROUPS, HOLDERS, ROWS, 128)
    own = lax.all_to_all(
        stack(owner_plan, held), ("win", "chan"), 0, 0, tiled=True, axis_index_groups=SAME_CORE
    )
    far = lax.ppermute(own, "win", CORE_SWAP)
    part, far_table, taper = begin(own, LAGS // GROUPS)
    return finish(part, far, far_table, taper)


def solution(mesh):
    return jax.shard_map(
        shards,
        mesh=mesh,
        in_specs=(P("win", "chan", None), P("win", "chan", None), P("win", "chan"), P()),
        out_specs=P(None, None, "chan", "win"),
        check_vma=False,
    )
```

```python
import math

import jax
import jax.numpy as jnp
from jax import lax
from jax.experimental import pallas as pl
from jax.experimental.pallas import tpu as pltpu
from jax.sharding import PartitionSpec as P

LAGS = 4096
STEPS = 6
FREQ = 512
SRC = 128
HOLDERS = 32
BLOCKS = 2 * FREQ // 128
SHARE = 3
LOCAL_WIN = 8
FINE = 4
ROWS = 72
GROUPS = 4
F32 = jnp.float32
BF16 = jnp.bfloat16
CORE_SWAP = [(0, 1), (1, 0), (2, 3), (3, 2)]


def params(mebibytes):
    return pltpu.CompilerParams(vmem_limit_bytes=mebibytes * 1024 * 1024)


def pack_kernel(mask_ref, re_ref, im_ref, rec_re_ref, rec_im_ref, out_ref, block):
    lane = lax.broadcasted_iota(jnp.int32, (1, 128), 1)
    usable = jnp.zeros((1, 128), F32)
    for w in range(LOCAL_WIN):
        for r in range(4):
            usable = jnp.where(lane == 4 * w + r, mask_ref[r, w].astype(F32), usable)
    block[:, 32:, :] = jnp.zeros((2, 96, 128), F32)
    low = lax.broadcasted_iota(jnp.int32, (128, 128), 0) % 8 < 4

    def split(first, second):
        down = pltpu.roll(second, 4, 0)
        up = pltpu.roll(first, 124, 0)
        return jnp.where(low, first, down), jnp.where(low, up, second)

    for b in range(2):
        lanes = slice(128 * b, 128 * b + 128)
        for part, ref in enumerate((rec_re_ref, rec_im_ref)):
            for w in range(LOCAL_WIN):
                block[part, 4 * w : 4 * w + 4, :] = ref[w, :, lanes].astype(F32)
        for core, tiles in enumerate(split(block[0].T * usable, block[1].T * usable)):
            out_ref[32 * core + 16 * b : 32 * core + 16 * b + 16, 64:, :] = tiles.reshape(16, 8, 128).astype(BF16)
        for part, ref in enumerate((re_ref, im_ref)):
            for w in range(0, LOCAL_WIN, 4):
                turned = [ref[w + k, :, lanes].astype(F32).T for k in range(4)]
                cores = zip(split(turned[0], turned[1]), split(turned[2], turned[3]))
                row = 32 * part + 4 * w
                for core, pair in enumerate(cores):
                    both = jnp.concatenate([tiles.reshape(16, 8, 128) for tiles in pair], axis=1)
                    out_ref[32 * core + 16 * b : 32 * core + 16 * b + 16, row : row + 16, :] = both.astype(BF16)


def pack(source_spectra, receiver_spectra, quality_mask):
    return pl.pallas_call(
        pack_kernel,
        grid=(2,),
        in_specs=[
            pl.BlockSpec(memory_space=pltpu.SMEM),
            pl.BlockSpec((LOCAL_WIN, SRC, 256), lambda b: (0, 0, b)),
            pl.BlockSpec((LOCAL_WIN, SRC, 256), lambda b: (0, 0, b + 2)),
            pl.BlockSpec((LOCAL_WIN, 4, 256), lambda b: (0, 0, b)),
            pl.BlockSpec((LOCAL_WIN, 4, 256), lambda b: (0, 0, b + 2)),
        ],
        out_specs=pl.BlockSpec((64, ROWS, 128), lambda b: (b, 0, 0)),
        out_shape=jax.ShapeDtypeStruct((GROUPS * HOLDERS, ROWS, 128), BF16),
        scratch_shapes=[pltpu.VMEM((2, 128, 128), F32)],
        compiler_params=params(60),
    )(quality_mask.T, source_spectra, source_spectra, receiver_spectra, receiver_spectra)


def stack_kernel(plan, held_ref, out_ref, spread, chosen, weights, tall):
    flat = held_ref[:, :, 64:, :].reshape(GROUPS * HOLDERS * 8, 128)
    row = lax.broadcasted_iota(jnp.int32, (128, 256), 0)
    lane = lax.broadcasted_iota(jnp.int32, (128, 256), 1)
    holder = lax.broadcasted_iota(jnp.int32, (HOLDERS, 8, 256), 0)
    here = lax.broadcasted_iota(jnp.int32, (HOLDERS, 8, 256), 2) % 128 // 4 == holder
    for w in range(0, LOCAL_WIN, 2):
        place = jnp.where(row == 4 * (w + lane // 128) + lane % 4, 1.0, 0.0).astype(BF16)
        tiled = jnp.dot(flat, place, preferred_element_type=F32).reshape(GROUPS, HOLDERS, 8, 256)
        for group in range(GROUPS):
            two = jnp.sum(jnp.where(here, tiled[group], 0.0), axis=0)
            for k in range(2):
                for part in range(2):
                    one = two[FINE * part : FINE * part + FINE, 128 * k : 128 * k + 128]
                    spread[group, pl.ds(LOCAL_WIN * part + w + k, FINE, stride=16), :] = one
    for i in range(FINE):
        real, imag = [], []
        for group in range(GROUPS):
            tile = spread[group, 16 * i : 16 * i + 16, :]
            real += [tile]
            imag += [-tile[8:], tile[:8]]
        both = jnp.concatenate([jnp.concatenate(real, axis=0), jnp.concatenate(imag, axis=0)], axis=1)
        weights[i] = both.T.astype(BF16)

    @pl.loop(0, STEPS, step=2)
    def _(step):
        for k in range(2):
            for group in range(GROUPS):
                chosen[k, group] = held_ref[group, plan[step + k], :64, :].astype(F32)
        for i in range(FINE):
            pair = [
                jnp.concatenate([chosen[k, group, pl.ds(i, 16, stride=FINE), :] for group in range(GROUPS)], axis=0)
                for k in range(2)
            ]
            block = jnp.concatenate(pair, axis=1).astype(BF16)
            both = jnp.dot(weights[i], block, preferred_element_type=F32)
            for k in range(2):
                tall[k, pl.ds(i, 128, stride=8), :] = both[:128, 128 * k : 128 * k + 128]
                tall[k, pl.ds(FINE + i, 128, stride=8), :] = both[128:, 128 * k : 128 * k + 128]
        for k in range(2):
            spectra = tall[k].reshape(HOLDERS, 32, 128).astype(BF16)
            for half in range(2):
                out_ref[2 * half + (step + k) // SHARE, :, lax.rem(step + k, SHARE)] = spectra


def stack(plan, held):
    return pl.pallas_call(
        stack_kernel,
        in_specs=[pl.BlockSpec(memory_space=pltpu.SMEM), pl.BlockSpec(memory_space=pltpu.VMEM)],
        out_shape=jax.ShapeDtypeStruct((GROUPS, HOLDERS, SHARE, 32, 128), BF16),
        scratch_shapes=[
            pltpu.VMEM((GROUPS, 64, 128), F32),
            pltpu.VMEM((2, GROUPS, 64, 128), F32),
            pltpu.VMEM((FINE, 256, 64), BF16),
            pltpu.VMEM((2, 1024, 128), F32),
        ],
        compiler_params=params(8),
    )(plan, held).reshape(GROUPS * HOLDERS, SHARE, 32, 128)


def arrange(ref, step, lhs):
    held = ref[:, step].astype(F32)
    for r in range(4):
        turned = held[:, 8 * r : 8 * r + 8, :].reshape(2 * FREQ, 128).T
        for b in range(BLOCKS):
            lhs[b, pl.ds(r, 128, stride=4), :] = turned[:, 128 * b : 128 * b + 128]


def rows(lhs):
    return jnp.concatenate([lhs[b].astype(BF16) for b in range(BLOCKS)], axis=1)


def fill_table(table_ref, taper_ref):
    count = taper_ref.shape[1]
    scale = 1.0 / math.sqrt(FREQ * LOCAL_WIN * GROUPS)
    start = lax.axis_index("win") * count
    shift = lax.broadcasted_iota(jnp.int32, (8, count), 1) + (start - LAGS // 2)
    index = lax.broadcasted_iota(jnp.int32, (8, count), 0)

    def waves(wave):
        angle = ((wave * shift) & (2 * LAGS - 1)).astype(F32) * (math.pi / LAGS)
        return jnp.cos(angle), jnp.sin(angle)

    high_cos, high_sin = waves(64 * index + 64)
    mid_cos, mid_sin = waves(8 * index)
    low_cos, low_sin = waves(index)
    high_cos, high_sin = high_cos * scale, high_sin * scale
    real = index < 4
    fine = []
    for h in range(2):
        cos = jnp.concatenate([low_cos[4 * h : 4 * h + 4]] * 2, axis=0)
        sin = jnp.concatenate([low_sin[4 * h : 4 * h + 4]] * 2, axis=0)
        fine.append((jnp.where(real, cos, -sin), jnp.where(real, -sin, -cos)))
    for a in range(8):
        for b in range(8):
            cos = high_cos[a : a + 1] * mid_cos[b : b + 1] - high_sin[a : a + 1] * mid_sin[b : b + 1]
            sin = high_sin[a : a + 1] * mid_cos[b : b + 1] + high_cos[a : a + 1] * mid_sin[b : b + 1]
            for h, (by_cos, by_sin) in enumerate(fine):
                row = 8 * ((2 * (a // 4) + h) * HOLDERS + 8 * (a % 4) + b)
                table_ref[row : row + 8, :] = (cos * by_cos + sin * by_sin).astype(BF16)
    position = lax.broadcasted_iota(jnp.int32, (1, count), 1) + start
    edge = jnp.minimum(position, LAGS - 1 - position) + 1
    taper_ref[...] = jnp.minimum(1.0, edge.astype(F32) / (LAGS // 16))


def project(held_ref, table_ref, taper_ref, out_ref, first, even, odd, ready, sems):
    count = table_ref.shape[1]
    lhs = (even, odd)

    def send(step, piece):
        sources = pl.ds(64 * piece, 64)
        return pltpu.make_async_copy(ready.at[step, sources], out_ref.at[first + step, sources], sems.at[step, piece])

    arrange(held_ref, 0, even)
    for step in range(SHARE):
        block = rows(lhs[step % 2])
        for piece in range(2):
            here = slice(256 * piece, 256 * piece + 256)
            for n in range(0, count, 256):
                lags = slice(n, n + 256)
                total = jnp.dot(block[here], table_ref[:, lags], preferred_element_type=F32) * taper_ref[:, lags]
                ready[step, 64 * piece : 64 * piece + 64, :, lags] = total.reshape(64, 4, 256).astype(BF16)
            send(step, piece).start()
        if step + 1 < SHARE:
            arrange(held_ref, step + 1, lhs[1 - step % 2])
    for step in range(SHARE):
        for piece in range(2):
            send(step, piece).wait()


def begin_kernel(own_ref, out_ref, table_ref, taper_ref, *scratch):
    fill_table(table_ref, taper_ref)
    project(own_ref, table_ref, taper_ref, out_ref, SHARE * (lax.axis_index("win") % 2), *scratch)


def finish_kernel(far_ref, table_ref, taper_ref, _, out_ref, *scratch):
    project(far_ref, table_ref, taper_ref, out_ref, SHARE * (1 - lax.axis_index("win") % 2), *scratch)


def settings(count):
    return dict(
        scratch_shapes=[
            pltpu.VMEM((BLOCKS, 512, 128), F32),
            pltpu.VMEM((BLOCKS, 512, 128), F32),
            pltpu.VMEM((SHARE, SRC, 4, count), BF16),
            pltpu.SemaphoreType.DMA((SHARE, 2)),
        ],
        compiler_params=params(16),
        cost_estimate=pl.CostEstimate(flops=SHARE * 2_000_000_000, bytes_accessed=10_000_000, transcendentals=0),
    )


def begin(own, count):
    return pl.pallas_call(
        begin_kernel,
        out_specs=[pl.BlockSpec(memory_space=pl.ANY)] + [pl.BlockSpec(memory_space=pltpu.VMEM)] * 2,
        out_shape=[
            jax.ShapeDtypeStruct((STEPS, SRC, 4, count), BF16),
            jax.ShapeDtypeStruct((2 * FREQ, count), BF16),
            jax.ShapeDtypeStruct((1, count), F32),
        ],
        **settings(count),
    )(own)


def finish(far, table, taper, out):
    vmem = pl.BlockSpec(memory_space=pltpu.VMEM)
    return pl.pallas_call(
        finish_kernel,
        in_specs=[vmem, vmem, vmem, pl.BlockSpec(memory_space=pl.ANY)],
        out_specs=pl.BlockSpec(memory_space=pl.ANY),
        out_shape=jax.ShapeDtypeStruct(out.shape, BF16),
        input_output_aliases={3: 0},
        **settings(table.shape[1]),
    )(far, table, taper, out)


def exchange(blocks):
    return lax.all_to_all(blocks, ("win", "chan"), 0, 0, tiled=True)


def shards(source_spectra, receiver_spectra, quality_mask, owner_plan):
    packed = pack(source_spectra, receiver_spectra, quality_mask)
    held = exchange(packed).reshape(GROUPS, HOLDERS, ROWS, 128)
    own = exchange(stack(owner_plan, held))
    far = lax.ppermute(own, "win", CORE_SWAP)
    out, table, taper = begin(own, LAGS // GROUPS)
    return finish(far, table, taper, out)


def solution(mesh):
    return jax.shard_map(
        shards,
        mesh=mesh,
        in_specs=(P("win", "chan", None), P("win", "chan", None), P("win", "chan"), P()),
        out_specs=P(None, None, "chan", "win"),
        check_vma=False,
    )
```

```python
import math

import jax
import jax.numpy as jnp
from jax import lax
from jax.experimental import pallas as pl
from jax.experimental.pallas import tpu as pltpu
from jax.sharding import PartitionSpec as P

LAGS = 4096
STEPS = 6
FREQ = 512
SRC = 128
HOLDERS = 32
BLOCKS = 2 * FREQ // 128
SHARE = 3
LOCAL_WIN = 8
FINE = 4
ROWS = 72
GROUPS = 4
F32 = jnp.float32
BF16 = jnp.bfloat16
CORE_SWAP = [(0, 1), (1, 0), (2, 3), (3, 2)]


def params(mebibytes):
    return pltpu.CompilerParams(vmem_limit_bytes=mebibytes * 1024 * 1024)


def pack_kernel(mask_ref, re_ref, im_ref, rec_re_ref, rec_im_ref, out_ref, block):
    lane = lax.broadcasted_iota(jnp.int32, (1, 128), 1)
    usable = jnp.zeros((1, 128), F32)
    for w in range(LOCAL_WIN):
        for r in range(4):
            usable = jnp.where(lane == 4 * w + r, mask_ref[r, w].astype(F32), usable)
    block[:, 32:, :] = jnp.zeros((2, 96, 128), F32)
    low = lax.broadcasted_iota(jnp.int32, (128, 128), 0) % 8 < 4

    def split(first, second):
        down = pltpu.roll(second, 4, 0)
        up = pltpu.roll(first, 124, 0)
        return jnp.where(low, first, down), jnp.where(low, up, second)

    for b in range(2):
        lanes = slice(128 * b, 128 * b + 128)
        for part, ref in enumerate((rec_re_ref, rec_im_ref)):
            for w in range(LOCAL_WIN):
                block[part, 4 * w : 4 * w + 4, :] = ref[w, :, lanes].astype(F32)
        for core, tiles in enumerate(split(block[0].T * usable, block[1].T * usable)):
            out_ref[32 * core + 16 * b : 32 * core + 16 * b + 16, 64:, :] = tiles.reshape(16, 8, 128).astype(BF16)
        for part, ref in enumerate((re_ref, im_ref)):
            for w in range(0, LOCAL_WIN, 4):
                turned = [ref[w + k, :, lanes].astype(F32).T for k in range(4)]
                cores = zip(split(turned[0], turned[1]), split(turned[2], turned[3]))
                row = 32 * part + 4 * w
                for core, pair in enumerate(cores):
                    both = jnp.concatenate([tiles.reshape(16, 8, 128) for tiles in pair], axis=1)
                    out_ref[32 * core + 16 * b : 32 * core + 16 * b + 16, row : row + 16, :] = both.astype(BF16)


def pack(source_spectra, receiver_spectra, quality_mask):
    return pl.pallas_call(
        pack_kernel,
        grid=(2,),
        in_specs=[
            pl.BlockSpec(memory_space=pltpu.SMEM),
            pl.BlockSpec((LOCAL_WIN, SRC, 256), lambda b: (0, 0, b)),
            pl.BlockSpec((LOCAL_WIN, SRC, 256), lambda b: (0, 0, b + 2)),
            pl.BlockSpec((LOCAL_WIN, 4, 256), lambda b: (0, 0, b)),
            pl.BlockSpec((LOCAL_WIN, 4, 256), lambda b: (0, 0, b + 2)),
        ],
        out_specs=pl.BlockSpec((64, ROWS, 128), lambda b: (b, 0, 0)),
        out_shape=pltpu.VMEM((GROUPS * HOLDERS, ROWS, 128), BF16),
        scratch_shapes=[pltpu.VMEM((2, 128, 128), F32)],
        compiler_params=params(58),
    )(quality_mask.T, source_spectra, source_spectra, receiver_spectra, receiver_spectra)


def stack_kernel(plan, held_ref, out_ref, spread, chosen, weights, tall):
    flat = held_ref[:, :, 64:, :].reshape(GROUPS * HOLDERS * 8, 128)
    row = lax.broadcasted_iota(jnp.int32, (128, 256), 0)
    lane = lax.broadcasted_iota(jnp.int32, (128, 256), 1)
    holder = lax.broadcasted_iota(jnp.int32, (HOLDERS, 8, 256), 0)
    here = lax.broadcasted_iota(jnp.int32, (HOLDERS, 8, 256), 2) % 128 // 4 == holder
    for w in range(0, LOCAL_WIN, 2):
        place = jnp.where(row == 4 * (w + lane // 128) + lane % 4, 1.0, 0.0).astype(BF16)
        tiled = jnp.dot(flat, place, preferred_element_type=F32).reshape(GROUPS, HOLDERS, 8, 256)
        for group in range(GROUPS):
            two = jnp.sum(jnp.where(here, tiled[group], 0.0), axis=0)
            for k in range(2):
                for part in range(2):
                    one = two[FINE * part : FINE * part + FINE, 128 * k : 128 * k + 128]
                    spread[group, pl.ds(LOCAL_WIN * part + w + k, FINE, stride=16), :] = one
    for i in range(FINE):
        real, imag = [], []
        for group in range(GROUPS):
            tile = spread[group, 16 * i : 16 * i + 16, :]
            real += [tile]
            imag += [-tile[8:], tile[:8]]
        both = jnp.concatenate([jnp.concatenate(real, axis=0), jnp.concatenate(imag, axis=0)], axis=1)
        weights[i] = both.T.astype(BF16)

    for step in range(0, STEPS, 2):
        for k in range(2):
            for group in range(GROUPS):
                chosen[k, group] = held_ref[group, plan[step + k], :64, :].astype(F32)
        for i in range(FINE):
            pair = [
                jnp.concatenate([chosen[k, group, pl.ds(i, 16, stride=FINE), :] for group in range(GROUPS)], axis=0)
                for k in range(2)
            ]
            block = jnp.concatenate(pair, axis=1).astype(BF16)
            both = jnp.dot(weights[i], block, preferred_element_type=F32)
            for k in range(2):
                tall[k, pl.ds(i, 128, stride=8), :] = both[:128, 128 * k : 128 * k + 128]
                tall[k, pl.ds(FINE + i, 128, stride=8), :] = both[128:, 128 * k : 128 * k + 128]
        for k in range(2):
            spectra = tall[k].reshape(HOLDERS, 32, 128).astype(BF16)
            for half in range(2):
                out_ref[2 * half + (step + k) // SHARE, :, (step + k) % SHARE] = spectra


def stack(plan, held):
    return pl.pallas_call(
        stack_kernel,
        in_specs=[pl.BlockSpec(memory_space=pltpu.SMEM), pl.BlockSpec(memory_space=pltpu.VMEM)],
        out_shape=jax.ShapeDtypeStruct((GROUPS, HOLDERS, SHARE, 32, 128), BF16),
        scratch_shapes=[
            pltpu.VMEM((GROUPS, 64, 128), F32),
            pltpu.VMEM((2, GROUPS, 64, 128), F32),
            pltpu.VMEM((FINE, 256, 64), BF16),
            pltpu.VMEM((2, 1024, 128), F32),
        ],
        compiler_params=params(8),
    )(plan, held).reshape(GROUPS * HOLDERS, SHARE, 32, 128)


def arrange(ref, step, lhs):
    held = ref[:, step].astype(F32)
    for r in range(4):
        turned = held[:, 8 * r : 8 * r + 8, :].reshape(2 * FREQ, 128).T
        for b in range(BLOCKS):
            lhs[b, pl.ds(r, 128, stride=4), :] = turned[:, 128 * b : 128 * b + 128]


def rows(lhs):
    return jnp.concatenate([lhs[b].astype(BF16) for b in range(BLOCKS)], axis=1)


def fill_table(table_ref, taper_ref):
    count = taper_ref.shape[1]
    scale = 1.0 / math.sqrt(FREQ * LOCAL_WIN * GROUPS)
    start = lax.axis_index("win") * count
    shift = lax.broadcasted_iota(jnp.int32, (8, count), 1) + (start - LAGS // 2)
    index = lax.broadcasted_iota(jnp.int32, (8, count), 0)

    def waves(wave):
        angle = ((wave * shift) & (2 * LAGS - 1)).astype(F32) * (math.pi / LAGS)
        return jnp.cos(angle), jnp.sin(angle)

    high_cos, high_sin = waves(64 * index + 64)
    mid_cos, mid_sin = waves(8 * index)
    low_cos, low_sin = waves(index)
    high_cos, high_sin = high_cos * scale, high_sin * scale
    real = index < 4
    fine = []
    for h in range(2):
        cos = jnp.concatenate([low_cos[4 * h : 4 * h + 4]] * 2, axis=0)
        sin = jnp.concatenate([low_sin[4 * h : 4 * h + 4]] * 2, axis=0)
        fine.append((jnp.where(real, cos, -sin), jnp.where(real, -sin, -cos)))
    for a in range(8):
        cos = high_cos[a : a + 1] * mid_cos - high_sin[a : a + 1] * mid_sin
        sin = high_sin[a : a + 1] * mid_cos + high_cos[a : a + 1] * mid_sin
        for h, (by_cos, by_sin) in enumerate(fine):
            for b in range(0, 8, 2):
                pair = [cos[k : k + 1] * by_cos + sin[k : k + 1] * by_sin for k in (b, b + 1)]
                row = 8 * ((2 * (a // 4) + h) * HOLDERS + 8 * (a % 4) + b)
                table_ref[row : row + 16, :] = jnp.concatenate(pair, axis=0).astype(BF16)
    position = lax.broadcasted_iota(jnp.int32, (1, count), 1) + start
    edge = jnp.minimum(position, LAGS - 1 - position) + 1
    taper_ref[...] = jnp.minimum(1.0, edge.astype(F32) / (LAGS // 16))


def project(held_ref, table_ref, taper_ref, out_ref, first, even, odd, ready, sems):
    count = table_ref.shape[1]
    lhs = (even, odd)

    def send(step, piece):
        sources = pl.ds(64 * piece, 64)
        return pltpu.make_async_copy(ready.at[step, sources], out_ref.at[first + step, sources], sems.at[step, piece])

    arrange(held_ref, 0, even)
    for step in range(SHARE):
        block = rows(lhs[step % 2])
        for piece in range(2):
            here = slice(256 * piece, 256 * piece + 256)
            for n in range(0, count, 256):
                lags = slice(n, n + 256)
                total = jnp.dot(block[here], table_ref[:, lags], preferred_element_type=F32) * taper_ref[:, lags]
                ready[step, 64 * piece : 64 * piece + 64, :, lags] = total.reshape(64, 4, 256).astype(BF16)
            send(step, piece).start()
        if step + 1 < SHARE:
            arrange(held_ref, step + 1, lhs[1 - step % 2])
    for step in range(SHARE):
        for piece in range(2):
            send(step, piece).wait()


def begin_kernel(own_ref, out_ref, table_ref, taper_ref, *scratch):
    fill_table(table_ref, taper_ref)
    project(own_ref, table_ref, taper_ref, out_ref, SHARE * (lax.axis_index("win") % 2), *scratch)


def finish_kernel(far_ref, table_ref, taper_ref, _, out_ref, *scratch):
    project(far_ref, table_ref, taper_ref, out_ref, SHARE * (1 - lax.axis_index("win") % 2), *scratch)


def settings(count):
    return dict(
        scratch_shapes=[
            pltpu.VMEM((BLOCKS, 512, 128), F32),
            pltpu.VMEM((BLOCKS, 512, 128), F32),
            pltpu.VMEM((SHARE, SRC, 4, count), BF16),
            pltpu.SemaphoreType.DMA((SHARE, 2)),
        ],
        compiler_params=params(16),
        cost_estimate=pl.CostEstimate(flops=SHARE * 2_000_000_000, bytes_accessed=10_000_000, transcendentals=0),
    )


def begin(own, count):
    return pl.pallas_call(
        begin_kernel,
        out_specs=[pl.BlockSpec(memory_space=pl.ANY)] + [pl.BlockSpec(memory_space=pltpu.VMEM)] * 2,
        out_shape=[
            jax.ShapeDtypeStruct((STEPS, SRC, 4, count), BF16),
            jax.ShapeDtypeStruct((2 * FREQ, count), BF16),
            jax.ShapeDtypeStruct((1, count), F32),
        ],
        **settings(count),
    )(own)


def finish(far, table, taper, out):
    vmem = pl.BlockSpec(memory_space=pltpu.VMEM)
    return pl.pallas_call(
        finish_kernel,
        in_specs=[vmem, vmem, vmem, pl.BlockSpec(memory_space=pl.ANY)],
        out_specs=pl.BlockSpec(memory_space=pl.ANY),
        out_shape=jax.ShapeDtypeStruct(out.shape, BF16),
        input_output_aliases={3: 0},
        **settings(table.shape[1]),
    )(far, table, taper, out)


def exchange(blocks):
    return lax.all_to_all(blocks, ("win", "chan"), 0, 0, tiled=True)


def shards(source_spectra, receiver_spectra, quality_mask, owner_plan):
    packed = pack(source_spectra, receiver_spectra, quality_mask)
    held = exchange(packed).reshape(GROUPS, HOLDERS, ROWS, 128)
    own = exchange(stack(owner_plan, held))
    far = lax.ppermute(own, "win", CORE_SWAP)
    out, table, taper = begin(own, LAGS // GROUPS)
    return finish(far, table, taper, out)


def solution(mesh):
    return jax.shard_map(
        shards,
        mesh=mesh,
        in_specs=(P("win", "chan", None), P("win", "chan", None), P("win", "chan"), P()),
        out_specs=P(None, None, "chan", "win"),
        check_vma=False,
    )
```

```python
import math

import jax
import jax.numpy as jnp
from jax import lax
from jax.experimental import pallas as pl
from jax.experimental.pallas import tpu as pltpu
from jax.sharding import PartitionSpec as P

LAGS = 4096
STEPS = 6
FREQ = 512
SRC = 128
HOLDERS = 32
BLOCKS = 2 * FREQ // 128
SHARE = 3
LOCAL_WIN = 8
FINE = 4
TILES = 17
GROUPS = 4
F32 = jnp.float32
BF16 = jnp.bfloat16
CORE_SWAP = [(0, 1), (1, 0), (2, 3), (3, 2)]


def params(mebibytes):
    return pltpu.CompilerParams(vmem_limit_bytes=mebibytes * 1024 * 1024)


def pack_kernel(mask_ref, re_ref, im_ref, rec_re_ref, rec_im_ref, out_ref, block):
    lane = lax.broadcasted_iota(jnp.int32, (1, 128), 1)
    usable = jnp.zeros((1, 128), F32)
    for w in range(LOCAL_WIN):
        for r in range(4):
            usable = jnp.where(lane % 32 == 4 * w + r, mask_ref[r, w].astype(F32), usable)
    block[64:, :] = jnp.zeros((64, 128), F32)

    def put(b, tile, turned):
        for core in range(2):
            chans = slice(32 * core + 16 * b, 32 * core + 16 * b + 16)
            out_ref[chans, tile] = turned.reshape(16, 2, 4, 128)[:, core].astype(BF16)

    for b in range(2):
        lanes = slice(128 * b, 128 * b + 128)
        for part, ref in enumerate((rec_re_ref, rec_im_ref)):
            for w in range(LOCAL_WIN):
                row = 32 * part + 4 * w
                block[row : row + 4, :] = ref[w, :, lanes].astype(F32)
        put(b, TILES - 1, block[...].T * usable)
        for part, ref in enumerate((re_ref, im_ref)):
            for w in range(LOCAL_WIN):
                put(b, LOCAL_WIN * part + w, ref[w, :, lanes].astype(F32).T)


def pack(source_spectra, receiver_spectra, quality_mask):
    return pl.pallas_call(
        pack_kernel,
        grid=(2,),
        in_specs=[
            pl.BlockSpec(memory_space=pltpu.SMEM),
            pl.BlockSpec((LOCAL_WIN, SRC, 256), lambda b: (0, 0, b)),
            pl.BlockSpec((LOCAL_WIN, SRC, 256), lambda b: (0, 0, b + 2)),
            pl.BlockSpec((LOCAL_WIN, 4, 256), lambda b: (0, 0, b)),
            pl.BlockSpec((LOCAL_WIN, 4, 256), lambda b: (0, 0, b + 2)),
        ],
        out_specs=pl.BlockSpec((64, TILES, 4, 128), lambda b: (b, 0, 0, 0)),
        out_shape=pltpu.VMEM((GROUPS * HOLDERS, TILES, 4, 128), BF16),
        scratch_shapes=[pltpu.VMEM((128, 128), F32)],
        compiler_params=params(58),
    )(quality_mask.T, source_spectra, source_spectra, receiver_spectra, receiver_spectra)


def stack_kernel(plan, held_ref, out_ref, spread, chosen, weights, tall):
    flat = held_ref[:, :, TILES - 1].astype(F32).reshape(GROUPS * HOLDERS * FINE, 128).astype(BF16)
    row = lax.broadcasted_iota(jnp.int32, (128, 256), 0)
    lane = lax.broadcasted_iota(jnp.int32, (128, 256), 1)
    holder = 2 * lax.broadcasted_iota(jnp.int32, (16, 8, 256), 0) + lax.broadcasted_iota(jnp.int32, (16, 8, 256), 1) // 4
    here = lax.broadcasted_iota(jnp.int32, (16, 8, 256), 2) % 128 // 4 == holder
    for k in range(0, 2 * LOCAL_WIN, 2):
        place = jnp.where(row == 4 * (k + lane // 128) + lane % 4, 1.0, 0.0).astype(BF16)
        tiled = jnp.dot(flat, place, preferred_element_type=F32).reshape(GROUPS, 16, 8, 256)
        for group in range(GROUPS):
            two = jnp.sum(jnp.where(here, tiled[group], 0.0), axis=0)
            two = two[:FINE] + two[FINE:]
            for j in range(2):
                spread[group, pl.ds(k + j, FINE, stride=16), :] = two[:, 128 * j : 128 * j + 128]
    for i in range(FINE):
        real, imag = [], []
        for group in range(GROUPS):
            tile = spread[group, 16 * i : 16 * i + 16, :]
            real += [tile]
            imag += [-tile[8:], tile[:8]]
        both = jnp.concatenate([jnp.concatenate(real, axis=0), jnp.concatenate(imag, axis=0)], axis=1)
        weights[i] = both.T.astype(BF16)

    for step in range(0, STEPS, 2):
        for k in range(2):
            for group in range(GROUPS):
                chosen[k, group] = held_ref[group, plan[step + k], :16].astype(F32).reshape(64, 128)
        for i in range(FINE):
            pair = [
                jnp.concatenate([chosen[k, group, pl.ds(i, 16, stride=FINE), :] for group in range(GROUPS)], axis=0)
                for k in range(2)
            ]
            block = jnp.concatenate(pair, axis=1).astype(BF16)
            both = jnp.dot(weights[i], block, preferred_element_type=F32)
            for k in range(2):
                tall[k, pl.ds(i, 128, stride=8), :] = both[:128, 128 * k : 128 * k + 128]
                tall[k, pl.ds(FINE + i, 128, stride=8), :] = both[128:, 128 * k : 128 * k + 128]
        for k in range(2):
            spectra = tall[k].reshape(HOLDERS, 32, 128).astype(BF16)
            for half in range(2):
                out_ref[2 * half + (step + k) // SHARE, :, (step + k) % SHARE] = spectra


def stack(plan, held):
    return pl.pallas_call(
        stack_kernel,
        in_specs=[pl.BlockSpec(memory_space=pltpu.SMEM), pl.BlockSpec(memory_space=pltpu.VMEM)],
        out_shape=jax.ShapeDtypeStruct((GROUPS, HOLDERS, SHARE, 32, 128), BF16),
        scratch_shapes=[
            pltpu.VMEM((GROUPS, 64, 128), F32),
            pltpu.VMEM((2, GROUPS, 64, 128), F32),
            pltpu.VMEM((FINE, 256, 64), BF16),
            pltpu.VMEM((2, 1024, 128), F32),
        ],
        compiler_params=params(8),
    )(plan, held).reshape(GROUPS * HOLDERS, SHARE, 32, 128)


def arrange(ref, step, lhs):
    held = ref[:, step].astype(F32)
    for r in range(4):
        turned = held[:, 8 * r : 8 * r + 8, :].reshape(2 * FREQ, 128).T
        for b in range(BLOCKS):
            lhs[b, pl.ds(r, 128, stride=4), :] = turned[:, 128 * b : 128 * b + 128]


def rows(lhs):
    return jnp.concatenate([lhs[b].astype(BF16) for b in range(BLOCKS)], axis=1)


def fill_table(table_ref, taper_ref):
    count = taper_ref.shape[1]
    scale = 1.0 / math.sqrt(FREQ * LOCAL_WIN * GROUPS)
    start = lax.axis_index("win") * count
    shift = lax.broadcasted_iota(jnp.int32, (8, count), 1) + (start - LAGS // 2)
    index = lax.broadcasted_iota(jnp.int32, (8, count), 0)

    def waves(wave):
        angle = ((wave * shift) & (2 * LAGS - 1)).astype(F32) * (math.pi / LAGS)
        return jnp.cos(angle), jnp.sin(angle)

    high_cos, high_sin = waves(64 * index + 64)
    mid_cos, mid_sin = waves(8 * index)
    low_cos, low_sin = waves(index)
    high_cos, high_sin = high_cos * scale, high_sin * scale
    real = index < 4
    fine = []
    for h in range(2):
        cos = jnp.concatenate([low_cos[4 * h : 4 * h + 4]] * 2, axis=0)
        sin = jnp.concatenate([low_sin[4 * h : 4 * h + 4]] * 2, axis=0)
        fine.append((jnp.where(real, cos, -sin), jnp.where(real, -sin, -cos)))
    for a in range(8):
        cos = high_cos[a : a + 1] * mid_cos - high_sin[a : a + 1] * mid_sin
        sin = high_sin[a : a + 1] * mid_cos + high_cos[a : a + 1] * mid_sin
        for h, (by_cos, by_sin) in enumerate(fine):
            for b in range(0, 8, 2):
                pair = [cos[k : k + 1] * by_cos + sin[k : k + 1] * by_sin for k in (b, b + 1)]
                row = 8 * ((2 * (a // 4) + h) * HOLDERS + 8 * (a % 4) + b)
                table_ref[row : row + 16, :] = jnp.concatenate(pair, axis=0).astype(BF16)
    position = lax.broadcasted_iota(jnp.int32, (1, count), 1) + start
    edge = jnp.minimum(position, LAGS - 1 - position) + 1
    taper_ref[...] = jnp.minimum(1.0, edge.astype(F32) / (LAGS // 16))


def project(held_ref, table_ref, taper_ref, out_ref, first, even, odd, ready, sems):
    count = table_ref.shape[1]
    lhs = (even, odd)

    def send(step, piece):
        sources = pl.ds(64 * piece, 64)
        return pltpu.make_async_copy(ready.at[step, sources], out_ref.at[first + step, sources], sems.at[step, piece])

    arrange(held_ref, 0, even)
    for step in range(SHARE):
        block = rows(lhs[step % 2])
        for piece in range(2):
            here = slice(256 * piece, 256 * piece + 256)
            for n in range(0, count, 256):
                lags = slice(n, n + 256)
                total = jnp.dot(block[here], table_ref[:, lags], preferred_element_type=F32) * taper_ref[:, lags]
                ready[step, 64 * piece : 64 * piece + 64, :, lags] = total.reshape(64, 4, 256).astype(BF16)
            send(step, piece).start()
        if step + 1 < SHARE:
            arrange(held_ref, step + 1, lhs[1 - step % 2])
    for step in range(SHARE):
        for piece in range(2):
            send(step, piece).wait()


def begin_kernel(own_ref, out_ref, table_ref, taper_ref, *scratch):
    fill_table(table_ref, taper_ref)
    project(own_ref, table_ref, taper_ref, out_ref, SHARE * (lax.axis_index("win") % 2), *scratch)


def finish_kernel(far_ref, table_ref, taper_ref, _, out_ref, *scratch):
    project(far_ref, table_ref, taper_ref, out_ref, SHARE * (1 - lax.axis_index("win") % 2), *scratch)


def settings(count):
    return dict(
        scratch_shapes=[
            pltpu.VMEM((BLOCKS, 512, 128), F32),
            pltpu.VMEM((BLOCKS, 512, 128), F32),
            pltpu.VMEM((SHARE, SRC, 4, count), BF16),
            pltpu.SemaphoreType.DMA((SHARE, 2)),
        ],
        compiler_params=params(16),
        cost_estimate=pl.CostEstimate(flops=SHARE * 2_000_000_000, bytes_accessed=10_000_000, transcendentals=0),
    )


def begin(own, count):
    return pl.pallas_call(
        begin_kernel,
        out_specs=[pl.BlockSpec(memory_space=pl.ANY)] + [pl.BlockSpec(memory_space=pltpu.VMEM)] * 2,
        out_shape=[
            jax.ShapeDtypeStruct((STEPS, SRC, 4, count), BF16),
            jax.ShapeDtypeStruct((2 * FREQ, count), BF16),
            jax.ShapeDtypeStruct((1, count), F32),
        ],
        **settings(count),
    )(own)


def finish(far, table, taper, out):
    vmem = pl.BlockSpec(memory_space=pltpu.VMEM)
    return pl.pallas_call(
        finish_kernel,
        in_specs=[vmem, vmem, vmem, pl.BlockSpec(memory_space=pl.ANY)],
        out_specs=pl.BlockSpec(memory_space=pl.ANY),
        out_shape=jax.ShapeDtypeStruct(out.shape, BF16),
        input_output_aliases={3: 0},
        **settings(table.shape[1]),
    )(far, table, taper, out)


def exchange(blocks):
    return lax.all_to_all(blocks, ("win", "chan"), 0, 0, tiled=True)


def shards(source_spectra, receiver_spectra, quality_mask, owner_plan):
    packed = pack(source_spectra, receiver_spectra, quality_mask)
    held = exchange(packed).reshape(GROUPS, HOLDERS, TILES, 4, 128)
    own = exchange(stack(owner_plan, held))
    far = lax.ppermute(own, "win", CORE_SWAP)
    out, table, taper = begin(own, LAGS // GROUPS)
    return finish(far, table, taper, out)


def solution(mesh):
    return jax.shard_map(
        shards,
        mesh=mesh,
        in_specs=(P("win", "chan", None), P("win", "chan", None), P("win", "chan"), P()),
        out_specs=P(None, None, "chan", "win"),
        check_vma=False,
    )
```

```python
import math

import jax
import jax.numpy as jnp
from jax import lax
from jax.experimental import pallas as pl
from jax.experimental.pallas import tpu as pltpu
from jax.sharding import PartitionSpec as P

LAGS = 4096
STEPS = 6
FREQ = 512
SRC = 128
HOLDERS = 32
BLOCKS = 2 * FREQ // 128
SHARE = 3
LOCAL_WIN = 8
FINE = 4
TILES = 17
GROUPS = 4
F32 = jnp.float32
BF16 = jnp.bfloat16
CORE_SWAP = [(0, 1), (1, 0), (2, 3), (3, 2)]


def params(mebibytes):
    return pltpu.CompilerParams(vmem_limit_bytes=mebibytes * 1024 * 1024)


def pack_kernel(mask_ref, re_ref, im_ref, rec_re_ref, rec_im_ref, out_ref, block):
    lane = lax.broadcasted_iota(jnp.int32, (1, 128), 1)
    usable = jnp.zeros((1, 128), F32)
    for w in range(LOCAL_WIN):
        for r in range(4):
            usable = jnp.where(lane % 32 == 4 * w + r, mask_ref[r, w].astype(F32), usable)
    block[64:, :] = jnp.zeros((64, 128), F32)

    def put(b, tile, turned):
        for core in range(2):
            chans = slice(32 * core + 16 * b, 32 * core + 16 * b + 16)
            out_ref[chans, tile] = turned.reshape(16, 2, 4, 128)[:, core].astype(BF16)

    for b in range(2):
        lanes = slice(128 * b, 128 * b + 128)
        for part, ref in enumerate((rec_re_ref, rec_im_ref)):
            for w in range(LOCAL_WIN):
                row = 32 * part + 4 * w
                block[row : row + 4, :] = ref[w, :, lanes].astype(F32)
        put(b, TILES - 1, block[...].T * usable)
        for part, ref in enumerate((re_ref, im_ref)):
            for w in range(LOCAL_WIN):
                put(b, LOCAL_WIN * part + w, ref[w, :, lanes].astype(F32).T)


def pack(source_spectra, receiver_spectra, quality_mask):
    return pl.pallas_call(
        pack_kernel,
        grid=(2,),
        in_specs=[
            pl.BlockSpec(memory_space=pltpu.SMEM),
            pl.BlockSpec((LOCAL_WIN, SRC, 256), lambda b: (0, 0, b)),
            pl.BlockSpec((LOCAL_WIN, SRC, 256), lambda b: (0, 0, b + 2)),
            pl.BlockSpec((LOCAL_WIN, 4, 256), lambda b: (0, 0, b)),
            pl.BlockSpec((LOCAL_WIN, 4, 256), lambda b: (0, 0, b + 2)),
        ],
        out_specs=pl.BlockSpec((64, TILES, 4, 128), lambda b: (b, 0, 0, 0)),
        out_shape=pltpu.VMEM((GROUPS * HOLDERS, TILES, 4, 128), BF16),
        scratch_shapes=[pltpu.VMEM((128, 128), F32)],
        compiler_params=params(58),
    )(quality_mask.T, source_spectra, source_spectra, receiver_spectra, receiver_spectra)


def stack_kernel(plan, held_ref, out_ref, spread, chosen, weights, tall):
    flat = held_ref[:, :, TILES - 1].astype(F32).reshape(GROUPS * HOLDERS * FINE, 128).astype(BF16)
    row = lax.broadcasted_iota(jnp.int32, (128, 256), 0)
    lane = lax.broadcasted_iota(jnp.int32, (128, 256), 1)
    holder = 2 * lax.broadcasted_iota(jnp.int32, (16, 8, 256), 0) + lax.broadcasted_iota(jnp.int32, (16, 8, 256), 1) // 4
    here = lax.broadcasted_iota(jnp.int32, (16, 8, 256), 2) % 128 // 4 == holder
    for k in range(0, 2 * LOCAL_WIN, 2):
        place = jnp.where(row == 4 * (k + lane // 128) + lane % 4, 1.0, 0.0).astype(BF16)
        tiled = jnp.dot(flat, place, preferred_element_type=F32).reshape(GROUPS, 16, 8, 256)
        for group in range(GROUPS):
            two = jnp.sum(jnp.where(here, tiled[group], 0.0), axis=0)
            two = two[:FINE] + two[FINE:]
            for j in range(2):
                spread[group, pl.ds(k + j, FINE, stride=16), :] = two[:, 128 * j : 128 * j + 128]
    for i in range(FINE):
        real, imag = [], []
        for group in range(GROUPS):
            tile = spread[group, 16 * i : 16 * i + 16, :]
            real += [tile]
            imag += [-tile[8:], tile[:8]]
        both = jnp.concatenate([jnp.concatenate(real, axis=0), jnp.concatenate(imag, axis=0)], axis=1)
        weights[i] = both.T.astype(BF16)

    for step in range(0, STEPS, 2):
        for k in range(2):
            for group in range(GROUPS):
                chosen[k, group] = held_ref[group, plan[step + k], :16].astype(F32).reshape(64, 128)
        for i in range(FINE):
            pair = [
                jnp.concatenate([chosen[k, group, pl.ds(i, 16, stride=FINE), :] for group in range(GROUPS)], axis=0)
                for k in range(2)
            ]
            block = jnp.concatenate(pair, axis=1).astype(BF16)
            both = jnp.dot(weights[i], block, preferred_element_type=F32)
            for k in range(2):
                tall[k, pl.ds(i, 128, stride=8), :] = both[:128, 128 * k : 128 * k + 128]
                tall[k, pl.ds(FINE + i, 128, stride=8), :] = both[128:, 128 * k : 128 * k + 128]
        for k in range(2):
            spectra = tall[k].reshape(HOLDERS, 32, 128).astype(BF16)
            for half in range(2):
                out_ref[2 * half + (step + k) // SHARE, :, (step + k) % SHARE] = spectra


def stack(plan, held):
    return pl.pallas_call(
        stack_kernel,
        in_specs=[pl.BlockSpec(memory_space=pltpu.SMEM), pl.BlockSpec(memory_space=pltpu.VMEM)],
        out_shape=jax.ShapeDtypeStruct((GROUPS, HOLDERS, SHARE, 32, 128), BF16),
        scratch_shapes=[
            pltpu.VMEM((GROUPS, 64, 128), F32),
            pltpu.VMEM((2, GROUPS, 64, 128), F32),
            pltpu.VMEM((FINE, 256, 64), BF16),
            pltpu.VMEM((2, 1024, 128), F32),
        ],
        compiler_params=params(8),
    )(plan, held).reshape(GROUPS * HOLDERS, SHARE, 32, 128)


def arrange(ref, step, lhs):
    held = ref[:, step].astype(F32)
    for r in range(4):
        turned = held[:, 8 * r : 8 * r + 8, :].reshape(2 * FREQ, 128).T
        for b in range(BLOCKS):
            lhs[b, pl.ds(r, 128, stride=4), :] = turned[:, 128 * b : 128 * b + 128]


def rows(lhs):
    return jnp.concatenate([lhs[b].astype(BF16) for b in range(BLOCKS)], axis=1)


def fill_table(table_ref, taper_ref):
    count = taper_ref.shape[1]
    scale = 1.0 / math.sqrt(FREQ * LOCAL_WIN * GROUPS)
    start = lax.axis_index("win") * count
    shift = lax.broadcasted_iota(jnp.int32, (8, count), 1) + (start - LAGS // 2)
    index = lax.broadcasted_iota(jnp.int32, (8, count), 0)

    def waves(wave):
        phase = (wave * shift) & (2 * LAGS - 1)
        quadrant = (phase + 1024) >> 11
        x = (phase - (quadrant << 11)).astype(F32) * (math.pi / LAGS)
        y = x * x
        cos = 1 + y * (-1 / 2 + y * (1 / 24 + y * (-1 / 720 + y * (1 / 40320 - y * (1 / 3628800)))))
        sin = x * (1 + y * (-1 / 6 + y * (1 / 120 + y * (-1 / 5040 + y * (1 / 362880)))))
        odd = (quadrant & 1) == 1
        first, second = jnp.where(odd, sin, cos), jnp.where(odd, cos, sin)
        return (
            jnp.where(((quadrant + 1) & 2) == 2, -first, first),
            jnp.where((quadrant & 2) == 2, -second, second),
        )

    high_cos, high_sin = waves(64 * index + 64)
    mid_cos, mid_sin = waves(8 * index)
    low_cos, low_sin = waves(index)
    high_cos, high_sin = high_cos * scale, high_sin * scale
    real = index < 4
    fine = []
    for h in range(2):
        cos = jnp.concatenate([low_cos[4 * h : 4 * h + 4]] * 2, axis=0)
        sin = jnp.concatenate([low_sin[4 * h : 4 * h + 4]] * 2, axis=0)
        fine.append((jnp.where(real, cos, -sin), jnp.where(real, -sin, -cos)))
    for a in range(8):
        cos = high_cos[a : a + 1] * mid_cos - high_sin[a : a + 1] * mid_sin
        sin = high_sin[a : a + 1] * mid_cos + high_cos[a : a + 1] * mid_sin
        for h, (by_cos, by_sin) in enumerate(fine):
            for b in range(0, 8, 2):
                pair = [cos[k : k + 1] * by_cos + sin[k : k + 1] * by_sin for k in (b, b + 1)]
                row = 8 * ((2 * (a // 4) + h) * HOLDERS + 8 * (a % 4) + b)
                table_ref[row : row + 16, :] = jnp.concatenate(pair, axis=0).astype(BF16)
    position = lax.broadcasted_iota(jnp.int32, (1, count), 1) + start
    edge = jnp.minimum(position, LAGS - 1 - position) + 1
    taper_ref[...] = jnp.minimum(1.0, edge.astype(F32) / (LAGS // 16))


def project(held_ref, table_ref, taper_ref, out_ref, first, even, odd, ready, sems):
    count = table_ref.shape[1]
    lhs = (even, odd)

    def send(step, piece):
        sources = pl.ds(64 * piece, 64)
        return pltpu.make_async_copy(ready.at[step, sources], out_ref.at[first + step, sources], sems.at[step, piece])

    arrange(held_ref, 0, even)
    for step in range(SHARE):
        block = rows(lhs[step % 2])
        for piece in range(2):
            here = slice(256 * piece, 256 * piece + 256)
            for n in range(0, count, 256):
                lags = slice(n, n + 256)
                total = jnp.dot(block[here], table_ref[:, lags], preferred_element_type=F32) * taper_ref[:, lags]
                ready[step, 64 * piece : 64 * piece + 64, :, lags] = total.reshape(64, 4, 256).astype(BF16)
            send(step, piece).start()
        if step + 1 < SHARE:
            arrange(held_ref, step + 1, lhs[1 - step % 2])
    for step in range(SHARE):
        for piece in range(2):
            send(step, piece).wait()


def begin_kernel(own_ref, out_ref, table_ref, taper_ref, *scratch):
    fill_table(table_ref, taper_ref)
    project(own_ref, table_ref, taper_ref, out_ref, SHARE * (lax.axis_index("win") % 2), *scratch)


def finish_kernel(far_ref, table_ref, taper_ref, _, out_ref, *scratch):
    project(far_ref, table_ref, taper_ref, out_ref, SHARE * (1 - lax.axis_index("win") % 2), *scratch)


def settings(count):
    return dict(
        scratch_shapes=[
            pltpu.VMEM((BLOCKS, 512, 128), F32),
            pltpu.VMEM((BLOCKS, 512, 128), F32),
            pltpu.VMEM((SHARE, SRC, 4, count), BF16),
            pltpu.SemaphoreType.DMA((SHARE, 2)),
        ],
        compiler_params=params(16),
        cost_estimate=pl.CostEstimate(flops=SHARE * 2_000_000_000, bytes_accessed=10_000_000, transcendentals=0),
    )


def begin(own, count):
    return pl.pallas_call(
        begin_kernel,
        out_specs=[pl.BlockSpec(memory_space=pl.ANY)] + [pl.BlockSpec(memory_space=pltpu.VMEM)] * 2,
        out_shape=[
            jax.ShapeDtypeStruct((STEPS, SRC, 4, count), BF16),
            jax.ShapeDtypeStruct((2 * FREQ, count), BF16),
            jax.ShapeDtypeStruct((1, count), F32),
        ],
        **settings(count),
    )(own)


def finish(far, table, taper, out):
    vmem = pl.BlockSpec(memory_space=pltpu.VMEM)
    return pl.pallas_call(
        finish_kernel,
        in_specs=[vmem, vmem, vmem, pl.BlockSpec(memory_space=pl.ANY)],
        out_specs=pl.BlockSpec(memory_space=pl.ANY),
        out_shape=jax.ShapeDtypeStruct(out.shape, BF16),
        input_output_aliases={3: 0},
        **settings(table.shape[1]),
    )(far, table, taper, out)


def exchange(blocks):
    return lax.all_to_all(blocks, ("win", "chan"), 0, 0, tiled=True)


def shards(source_spectra, receiver_spectra, quality_mask, owner_plan):
    packed = pack(source_spectra, receiver_spectra, quality_mask)
    held = exchange(packed).reshape(GROUPS, HOLDERS, TILES, 4, 128)
    own = exchange(stack(owner_plan, held))
    far = lax.ppermute(own, "win", CORE_SWAP)
    out, table, taper = begin(own, LAGS // GROUPS)
    return finish(far, table, taper, out)


def solution(mesh):
    return jax.shard_map(
        shards,
        mesh=mesh,
        in_specs=(P("win", "chan", None), P("win", "chan", None), P("win", "chan"), P()),
        out_specs=P(None, None, "chan", "win"),
        check_vma=False,
    )
```

```python
import math

import jax
import jax.numpy as jnp
from jax import lax
from jax.experimental import pallas as pl
from jax.experimental.pallas import tpu as pltpu
from jax.sharding import PartitionSpec as P

LAGS = 4096
STEPS = 6
FREQ = 512
SRC = 128
HOLDERS = 32
BLOCKS = 2 * FREQ // 128
SHARE = 3
LOCAL_WIN = 8
FINE = 4
TILES = 17
GROUPS = 4
F32 = jnp.float32
BF16 = jnp.bfloat16
CORE_SWAP = [(0, 1), (1, 0), (2, 3), (3, 2)]


def params(mebibytes):
    return pltpu.CompilerParams(vmem_limit_bytes=mebibytes * 1024 * 1024)


def pack_kernel(mask_ref, re_ref, im_ref, rec_re_ref, rec_im_ref, out_ref, block):
    lane = lax.broadcasted_iota(jnp.int32, (1, 128), 1)
    usable = jnp.zeros((1, 128), F32)
    for w in range(LOCAL_WIN):
        for r in range(4):
            usable = jnp.where(lane % 32 == 4 * w + r, mask_ref[r, w].astype(F32), usable)
    block[64:, :] = jnp.zeros((64, 128), F32)

    def put(b, tile, turned):
        for core in range(2):
            chans = slice(32 * core + 16 * b, 32 * core + 16 * b + 16)
            out_ref[chans, tile] = turned.reshape(16, 2, 4, 128)[:, core].astype(BF16)

    for b in range(2):
        lanes = slice(128 * b, 128 * b + 128)
        for part, ref in enumerate((rec_re_ref, rec_im_ref)):
            for w in range(LOCAL_WIN):
                row = 32 * part + 4 * w
                block[row : row + 4, :] = ref[w, :, lanes].astype(F32)
        put(b, TILES - 1, block[...].T * usable)
        for part, ref in enumerate((re_ref, im_ref)):
            for w in range(LOCAL_WIN):
                put(b, LOCAL_WIN * part + w, ref[w, :, lanes].astype(F32).T)


def pack(source_spectra, receiver_spectra, quality_mask):
    return pl.pallas_call(
        pack_kernel,
        grid=(2,),
        in_specs=[
            pl.BlockSpec(memory_space=pltpu.SMEM),
            pl.BlockSpec((LOCAL_WIN, SRC, 256), lambda b: (0, 0, b)),
            pl.BlockSpec((LOCAL_WIN, SRC, 256), lambda b: (0, 0, b + 2)),
            pl.BlockSpec((LOCAL_WIN, 4, 256), lambda b: (0, 0, b)),
            pl.BlockSpec((LOCAL_WIN, 4, 256), lambda b: (0, 0, b + 2)),
        ],
        out_specs=pl.BlockSpec((64, TILES, 4, 128), lambda b: (b, 0, 0, 0)),
        out_shape=pltpu.VMEM((GROUPS * HOLDERS, TILES, 4, 128), BF16),
        scratch_shapes=[pltpu.VMEM((128, 128), F32)],
        compiler_params=params(58),
    )(quality_mask.T, source_spectra, source_spectra, receiver_spectra, receiver_spectra)


def stack_kernel(plan, held_ref, out_ref, spread, chosen, weights, tall):
    flat = held_ref[:, :, TILES - 1].astype(F32).reshape(GROUPS * HOLDERS * FINE, 128).astype(BF16)
    row = lax.broadcasted_iota(jnp.int32, (128, 256), 0)
    lane = lax.broadcasted_iota(jnp.int32, (128, 256), 1)
    holder = 2 * lax.broadcasted_iota(jnp.int32, (16, 8, 256), 0) + lax.broadcasted_iota(jnp.int32, (16, 8, 256), 1) // 4
    here = lax.broadcasted_iota(jnp.int32, (16, 8, 256), 2) % 128 // 4 == holder
    for k in range(0, 2 * LOCAL_WIN, 2):
        place = jnp.where(row == 4 * (k + lane // 128) + lane % 4, 1.0, 0.0).astype(BF16)
        tiled = jnp.dot(flat, place, preferred_element_type=F32).reshape(GROUPS, 16, 8, 256)
        for group in range(GROUPS):
            two = jnp.sum(jnp.where(here, tiled[group], 0.0), axis=0)
            two = two[:FINE] + two[FINE:]
            for j in range(2):
                spread[group, pl.ds(k + j, FINE, stride=16), :] = two[:, 128 * j : 128 * j + 128]
    for i in range(FINE):
        real, imag = [], []
        for group in range(GROUPS):
            tile = spread[group, 16 * i : 16 * i + 16, :]
            real += [tile]
            imag += [-tile[8:], tile[:8]]
        both = jnp.concatenate([jnp.concatenate(real, axis=0), jnp.concatenate(imag, axis=0)], axis=1)
        weights[i] = both.T.astype(BF16)

    for step in range(0, STEPS, 2):
        for k in range(2):
            for group in range(GROUPS):
                chosen[k, group] = held_ref[group, plan[step + k], :16].astype(F32).reshape(64, 128)
        for i in range(FINE):
            pair = [
                jnp.concatenate([chosen[k, group, pl.ds(i, 16, stride=FINE), :] for group in range(GROUPS)], axis=0)
                for k in range(2)
            ]
            block = jnp.concatenate(pair, axis=1).astype(BF16)
            both = jnp.dot(weights[i], block, preferred_element_type=F32)
            for k in range(2):
                tall[k, pl.ds(i, 128, stride=8), :] = both[:128, 128 * k : 128 * k + 128]
                tall[k, pl.ds(FINE + i, 128, stride=8), :] = both[128:, 128 * k : 128 * k + 128]
        for k in range(2):
            spectra = tall[k].reshape(HOLDERS, 32, 128).astype(BF16)
            for half in range(2):
                out_ref[2 * half + (step + k) // SHARE, :, (step + k) % SHARE] = spectra


def stack(plan, held):
    return pl.pallas_call(
        stack_kernel,
        in_specs=[pl.BlockSpec(memory_space=pltpu.SMEM), pl.BlockSpec(memory_space=pltpu.VMEM)],
        out_shape=jax.ShapeDtypeStruct((GROUPS, HOLDERS, SHARE, 32, 128), BF16),
        scratch_shapes=[
            pltpu.VMEM((GROUPS, 64, 128), F32),
            pltpu.VMEM((2, GROUPS, 64, 128), F32),
            pltpu.VMEM((FINE, 256, 64), BF16),
            pltpu.VMEM((2, 1024, 128), F32),
        ],
        compiler_params=params(8),
    )(plan, held).reshape(GROUPS * HOLDERS, SHARE, 32, 128)


def arrange(ref, step, lhs):
    held = ref[:, step].astype(F32)
    for r in range(4):
        turned = held[:, 8 * r : 8 * r + 8, :].reshape(2 * FREQ, 128).T
        for b in range(BLOCKS):
            lhs[b, pl.ds(r, 128, stride=4), :] = turned[:, 128 * b : 128 * b + 128]


def rows(lhs):
    return jnp.concatenate([lhs[b].astype(BF16) for b in range(BLOCKS)], axis=1)


def fill_table(table_ref, taper_ref):
    count = taper_ref.shape[1]
    scale = 1.0 / math.sqrt(FREQ * LOCAL_WIN * GROUPS)
    start = lax.axis_index("win") * count
    shift = lax.broadcasted_iota(jnp.int32, (8, count), 1) + (start - LAGS // 2)
    index = lax.broadcasted_iota(jnp.int32, (8, count), 0)

    def waves(wave):
        phase = (wave * shift) & (2 * LAGS - 1)
        quadrant = (phase + 1024) >> 11
        x = (phase - (quadrant << 11)).astype(F32) * (math.pi / LAGS)
        y = x * x
        cos = 1 + y * (-1 / 2 + y * (1 / 24 + y * (-1 / 720 + y * (1 / 40320 - y * (1 / 3628800)))))
        sin = x * (1 + y * (-1 / 6 + y * (1 / 120 + y * (-1 / 5040 + y * (1 / 362880)))))
        odd = (quadrant & 1) == 1
        first, second = jnp.where(odd, sin, cos), jnp.where(odd, cos, sin)
        return (
            jnp.where(((quadrant + 1) & 2) == 2, -first, first),
            jnp.where((quadrant & 2) == 2, -second, second),
        )

    high_cos, high_sin = waves(64 * index + 64)
    mid_cos, mid_sin = waves(8 * index)
    low_cos, low_sin = waves(index)
    high_cos, high_sin = high_cos * scale, high_sin * scale
    real = index < 4
    fine = []
    for h in range(2):
        cos = jnp.concatenate([low_cos[4 * h : 4 * h + 4]] * 2, axis=0)
        sin = jnp.concatenate([low_sin[4 * h : 4 * h + 4]] * 2, axis=0)
        fine.append((jnp.where(real, cos, -sin), jnp.where(real, -sin, -cos)))
    for a in range(8):
        cos = high_cos[a : a + 1] * mid_cos - high_sin[a : a + 1] * mid_sin
        sin = high_sin[a : a + 1] * mid_cos + high_cos[a : a + 1] * mid_sin
        for h, (by_cos, by_sin) in enumerate(fine):
            for b in range(0, 8, 2):
                pair = [cos[k : k + 1] * by_cos + sin[k : k + 1] * by_sin for k in (b, b + 1)]
                row = 8 * ((2 * (a // 4) + h) * HOLDERS + 8 * (a % 4) + b)
                table_ref[row : row + 16, :] = jnp.concatenate(pair, axis=0).astype(BF16)
    position = lax.broadcasted_iota(jnp.int32, (1, count), 1) + start
    edge = jnp.minimum(position, LAGS - 1 - position) + 1
    taper_ref[...] = jnp.minimum(1.0, edge.astype(F32) / (LAGS // 16))


def project(held_ref, table_ref, taper_ref, out_ref, first, even, odd, ready, sems):
    count = table_ref.shape[1]
    lhs = (even, odd)

    cuts = [[0, 64, 128]] * (SHARE - 1) + [[0, 64, 96, 128]]

    def send(step, piece):
        at, end = cuts[step][piece : piece + 2]
        sources = pl.ds(at, end - at)
        return pltpu.make_async_copy(ready.at[step, sources], out_ref.at[first + step, sources], sems.at[step, piece])

    arrange(held_ref, 0, even)
    for step in range(SHARE):
        block = rows(lhs[step % 2])
        for piece in range(len(cuts[step]) - 1):
            at, end = cuts[step][piece : piece + 2]
            for n in range(0, count, 256):
                lags = slice(n, n + 256)
                total = jnp.dot(block[4 * at : 4 * end], table_ref[:, lags], preferred_element_type=F32)
                total = (total * taper_ref[:, lags]).reshape(end - at, 4, 256)
                ready[step, at:end, :, lags] = total.astype(BF16)
            send(step, piece).start()
        if step + 1 < SHARE:
            arrange(held_ref, step + 1, lhs[1 - step % 2])
    for step in range(SHARE):
        for piece in range(len(cuts[step]) - 1):
            send(step, piece).wait()


def begin_kernel(own_ref, out_ref, table_ref, taper_ref, *scratch):
    fill_table(table_ref, taper_ref)
    project(own_ref, table_ref, taper_ref, out_ref, SHARE * (lax.axis_index("win") % 2), *scratch)


def finish_kernel(far_ref, table_ref, taper_ref, _, out_ref, *scratch):
    project(far_ref, table_ref, taper_ref, out_ref, SHARE * (1 - lax.axis_index("win") % 2), *scratch)


def settings(count):
    return dict(
        scratch_shapes=[
            pltpu.VMEM((BLOCKS, 512, 128), F32),
            pltpu.VMEM((BLOCKS, 512, 128), F32),
            pltpu.VMEM((SHARE, SRC, 4, count), BF16),
            pltpu.SemaphoreType.DMA((SHARE, 3)),
        ],
        compiler_params=params(16),
        cost_estimate=pl.CostEstimate(flops=SHARE * 2_000_000_000, bytes_accessed=10_000_000, transcendentals=0),
    )


def begin(own, count):
    return pl.pallas_call(
        begin_kernel,
        out_specs=[pl.BlockSpec(memory_space=pl.ANY)] + [pl.BlockSpec(memory_space=pltpu.VMEM)] * 2,
        out_shape=[
            jax.ShapeDtypeStruct((STEPS, SRC, 4, count), BF16),
            jax.ShapeDtypeStruct((2 * FREQ, count), BF16),
            jax.ShapeDtypeStruct((1, count), F32),
        ],
        **settings(count),
    )(own)


def finish(far, table, taper, out):
    vmem = pl.BlockSpec(memory_space=pltpu.VMEM)
    return pl.pallas_call(
        finish_kernel,
        in_specs=[vmem, vmem, vmem, pl.BlockSpec(memory_space=pl.ANY)],
        out_specs=pl.BlockSpec(memory_space=pl.ANY),
        out_shape=jax.ShapeDtypeStruct(out.shape, BF16),
        input_output_aliases={3: 0},
        **settings(table.shape[1]),
    )(far, table, taper, out)


def exchange(blocks):
    return lax.all_to_all(blocks, ("win", "chan"), 0, 0, tiled=True)


def shards(source_spectra, receiver_spectra, quality_mask, owner_plan):
    packed = pack(source_spectra, receiver_spectra, quality_mask)
    held = exchange(packed).reshape(GROUPS, HOLDERS, TILES, 4, 128)
    own = exchange(stack(owner_plan, held))
    far = lax.ppermute(own, "win", CORE_SWAP)
    out, table, taper = begin(own, LAGS // GROUPS)
    return finish(far, table, taper, out)


def solution(mesh):
    return jax.shard_map(
        shards,
        mesh=mesh,
        in_specs=(P("win", "chan", None), P("win", "chan", None), P("win", "chan"), P()),
        out_specs=P(None, None, "chan", "win"),
        check_vma=False,
    )
```
